256 devices in a mesh: form: 64 (over z, x, core), focus: 4 (over y).
Axes of the slice: x: 4, y: 4, z: 8, core: 2. Of those that a mesh axis runs over, the one named last changes fastest.
Arguments:
- echoes: bfloat16 [2, 8192, 32768], P(None, ('form', 'focus')), may hold values from -6 to 6
- scale_rate: float32 [8192], P(('form', 'focus')), may hold values from 8 to 40
- migration: float32 [8192], P(('form', 'focus')), may hold values from -48 to 48
- range_phase: float32 [32768], replicated, may hold values from -3.140625 to 3.140625
- azimuth_rate: float32 [32768], P(('form', 'focus')), may hold values from 40 to 400
- bright_columns: int32 [64, 32], P('form'), may hold values from 0 to 511, as said below
- line_block: int32 [64, 32, 1], P('form'), may hold values from 0 to 255
- line_center: int32 [64, 32], P('form'), may hold values from 0 to 8191
Outputs:
- focused_image: bfloat16 [2, 8192, 32768], P(None, None, ('form', 'focus'))
- phase_map: float32 [256, 256], P(('form', 'focus'))
The draws below stay inside these ranges and needn't reach their ends.
Inputs may be any that keep to these rules, and one draw needn't show every extreme that they name: bright_columns[j, i] counts among the 512 range columns of form group j; columns may repeat. `line_block`: every map row is fed by at least one line.
All inputs are finite; a program needn't handle non-finite values.
Results may differ from the reference program's by a relative error of at most 0.02.
Values may be sent and summed in bfloat16 or wider, within the bound.
A program may use at most 128 MiB of HBM per device.

```python
import math
import jax
import jax.numpy as jnp
from jax import lax

A1 = 64
A2 = 128
R1 = 256
R2 = 128
AZ = 8192
RG = 32768
RC = 128
LG = 32
NBLK = 256
MAZ = 256
N_FORM = 64
N_FOCUS = 4


def draw_bright_columns(key, part):
    key = jax.random.fold_in(key, 7)
    subkeys = jax.random.split(key, 5)
    favored = jax.random.randint(subkeys[0], (N_FORM, 1), 0, N_FOCUS)
    solid = jax.random.randint(subkeys[1], (N_FORM, 1), 0, 4) == 0
    mixing = jax.random.randint(subkeys[2], (N_FORM, LG), 0, 8) < 5
    scatter_to = jax.random.randint(subkeys[3], (N_FORM, LG), 0, N_FOCUS)
    holder = jnp.where(solid | mixing, favored, scatter_to)
    offset = jax.random.randint(subkeys[4], (N_FORM, LG), 0, RC)
    return (holder * RC + offset).astype(jnp.int32)


def touch_ends(array, stream_key, least, high):
    spot = [jax.random.randint(jax.random.fold_in(stream_key, axis), (), 0, length) for axis, length in enumerate(array.shape)]
    main_axis = array.shape.index(max(array.shape))
    next_to = spot[:main_axis] + [(spot[main_axis] + 1) % array.shape[main_axis]] + spot[main_axis + 1:]
    return array.at[tuple(spot)].set(least).at[tuple(next_to)].set(high)


def block_levels(stream_key, shape, cuts, smallest, largest):
    level, own = 1.0, jax.random.fold_in(stream_key, 6)
    for dim, parts in cuts:
        heights = jnp.exp(jax.random.uniform(jax.random.fold_in(own, dim), (parts,), jnp.float32, smallest / len(cuts), largest / len(cuts)))
        level = level * jnp.repeat(heights, shape[dim] // parts).reshape([-1 if axis == dim else 1 for axis in range(len(shape))])
    return level


def choose_distinct(key, rows, count, top, lift):
    sequence = jax.random.permutation(jax.random.fold_in(key, 1), count)
    pull = sequence
    for power in range(3):
        pull = pull * pull // count
    pull = pull * lift // count
    chance = jax.random.randint(jax.random.fold_in(key, 2), (rows, count), 0, 4096) + pull
    sure = jax.random.permutation(jax.random.fold_in(key, 3), rows)[jnp.arange(count) % rows]
    chance = jnp.where(jnp.arange(rows)[:, None] == sure[None, :], 1 << 14, chance)
    priority = chance * count + jnp.arange(count)
    return lax.top_k(priority.astype(jnp.int32), top)[1].astype(jnp.int32)


def centred(own_key, extent, width, bound, shards=(), held_as=jnp.bfloat16):
    factor_of = block_levels(own_key, extent, shards, -0.22, 0.18) if shards else 1.0
    values = jax.random.normal(own_key, extent, jnp.float32) * width * factor_of
    return jnp.minimum(jnp.maximum(values, -bound), bound).astype(held_as)


def setup_inputs(seed: int = 0) -> dict:
    key_list = jax.random.split(jax.random.key(seed), 9)
    return {
        "echoes": centred(key_list[0], (2, AZ, RG), 1.0, 6.0, ((1, 256),)),
        "scale_rate": jnp.clip(8.0 + 32.0 * jax.random.uniform(key_list[1], (AZ,), jnp.float32) ** block_levels(key_list[1], (AZ,), ((0, 256),), -0.2, 0.2), 8.0, 40.0),
        "migration": jnp.clip(jax.random.uniform(key_list[2], (AZ,), jnp.float32, -48.0, 48.0) * block_levels(key_list[2], (AZ,), ((0, 256),), -0.4, 0.0), -48.0, 48.0),
        "range_phase": jnp.clip(jax.random.uniform(key_list[3], (RG,), jnp.float32, -3.140625, 3.140625), -3.140625, 3.140625),
        "azimuth_rate": jnp.clip(40.0 + 360.0 * jax.random.uniform(key_list[4], (RG,), jnp.float32) ** block_levels(key_list[4], (RG,), ((0, 256),), -0.2, 0.2), 40.0, 400.0),
        "bright_columns": draw_bright_columns(jax.random.fold_in(key_list[8], 71), 0),
        "line_block": choose_distinct(key_list[6], N_FORM * LG, NBLK, 1, 32).reshape((N_FORM, LG, 1)),
        "line_center": touch_ends(jax.random.randint(key_list[7], (N_FORM, LG), 0, AZ), jax.random.fold_in(key_list[7], 1), 0, AZ - 1).astype(jnp.int32),
    }


TWO_PI = 2.0 * math.pi
EPSILON = 1e-06

def section_table(factor, signum):
    indices = jnp.arange(factor, dtype=jnp.int32)
    products = indices[:, None] * indices[None, :] % factor
    angles = signum * TWO_PI / factor * products.astype(jnp.float32)
    scaling = 1.0 / math.sqrt(factor)
    cosine = jnp.cos(angles) * scaling
    sine_part = jnp.sin(angles) * scaling
    upper_rows = jnp.stack([cosine, -sine_part], axis=1)
    lower_rows = jnp.stack([sine_part, cosine], axis=1)
    return jnp.stack([upper_rows, lower_rows], axis=0).astype(jnp.bfloat16)

def twiddle_pair(outer_size, inner_size, modulus, signum):
    first_idx = jnp.arange(outer_size, dtype=jnp.int32)[:, None]
    second_idx = jnp.arange(inner_size, dtype=jnp.int32)[None, :]
    angles = signum * TWO_PI / modulus * (first_idx * second_idx % modulus).astype(jnp.float32)
    return (jnp.cos(angles), jnp.sin(angles))

def rotate(real_part, imag_part, cosine, sine_part):
    return (real_part * cosine - imag_part * sine_part, real_part * sine_part + imag_part * cosine)

def rounded(pair):
    return jnp.stack([pair[0], pair[1]]).astype(jnp.bfloat16)

def mix(pattern, matrix, values):
    return jnp.einsum(pattern, matrix.astype(jnp.float32), values.astype(jnp.float32), precision=lax.Precision.HIGHEST)

def forward_split(values, outer_size, inner_size, ordered):
    modulus = outer_size * inner_size
    first_section = mix('akcn,clnq->alkq', section_table(outer_size, -1.0), values)
    cosine, sine_part = twiddle_pair(outer_size, inner_size, modulus, -1.0)
    twisted = rounded(rotate(first_section[0], first_section[1], cosine[None], sine_part[None]))
    if ordered:
        return mix('apcq,clkq->alpk', section_table(inner_size, -1.0), twisted)
    return mix('apcq,clkq->alkp', section_table(inner_size, -1.0), twisted)

def range_lines(echo_part, rate_part, shift_part, range_phase):
    line_count = echo_part.shape[1]
    length = R1 * R2
    offsets = (jnp.arange(length, dtype=jnp.int32) - length // 2).astype(jnp.float32) / length
    angles = rate_part[:, None] * (offsets * offsets)[None, :]
    chirped = rounded(rotate(echo_part[0].astype(jnp.float32), echo_part[1].astype(jnp.float32), jnp.cos(angles), jnp.sin(angles)))
    first_section = mix('akcn,clnq->aklq', section_table(R1, -1.0), chirped.reshape(2, line_count, R1, R2))
    cosine, sine_part = twiddle_pair(R1, R2, length, -1.0)
    twisted = rounded(rotate(first_section[0], first_section[1], cosine[:, None, :], sine_part[:, None, :]))
    spectrum = mix('apcq,cklq->klap', section_table(R2, -1.0), twisted)
    freq_bins = jnp.arange(R1, dtype=jnp.int32)[:, None] + R1 * jnp.arange(R2, dtype=jnp.int32)[None, :]
    signed = jnp.where(freq_bins >= length // 2, freq_bins - length, freq_bins).astype(jnp.float32)
    phases = range_phase.reshape(R2, R1).T[:, None, :] + TWO_PI / length * signed[:, None, :] * shift_part[None, :, None]
    matched = rounded(rotate(spectrum[:, :, 0], spectrum[:, :, 1], jnp.cos(phases), -jnp.sin(phases)))
    back_section = mix('aqcp,cklp->klaq', section_table(R2, 1.0), matched)
    cosine, sine_part = twiddle_pair(R1, R2, length, 1.0)
    twisted = rounded(rotate(back_section[:, :, 0], back_section[:, :, 1], cosine[:, None, :], sine_part[:, None, :]))
    restored = mix('anck,cklq->anlq', section_table(R1, 1.0), twisted).astype(jnp.bfloat16)
    return jnp.transpose(restored, (0, 2, 1, 3)).reshape(2, line_count, length)

def azimuth_columns(columns, rate_part):
    col_width = columns.shape[2]
    modulus = A1 * A2
    shaped = columns.reshape(2, A1, A2, col_width)
    first_section = mix('akcm,cmqr->akqr', section_table(A1, -1.0), shaped)
    cosine, sine_part = twiddle_pair(A1, A2, modulus, -1.0)
    twisted = rounded(rotate(first_section[0], first_section[1], cosine[:, :, None], sine_part[:, :, None]))
    doppler = mix('apcq,ckqr->apkr', section_table(A2, -1.0), twisted)
    freq_bins = A1 * jnp.arange(A2, dtype=jnp.int32)[:, None] + jnp.arange(A1, dtype=jnp.int32)[None, :]
    signed = jnp.where(freq_bins >= modulus // 2, freq_bins - modulus, freq_bins).astype(jnp.float32) / modulus
    angles = (signed * signed)[:, :, None] * rate_part[None, None, :]
    history = rounded(rotate(doppler[0], doppler[1], jnp.cos(angles), -jnp.sin(angles)))
    first_back = mix('amcq,cqkr->amkr', section_table(A2, 1.0), history)
    cosine, sine_part = twiddle_pair(A1, A2, modulus, 1.0)
    twisted = rounded(rotate(first_back[0], first_back[1], cosine.T[:, :, None], sine_part.T[:, :, None]))
    restored = mix('anck,cmkr->anmr', section_table(A1, 1.0), twisted)
    return restored.reshape(2, modulus, col_width).astype(jnp.bfloat16)

def taper(centers, modulus):
    positions = jnp.arange(modulus, dtype=jnp.int32)
    offsets = (positions - centers[..., None]) % modulus
    distance = jnp.minimum(offsets, modulus - offsets)
    return jnp.maximum(1.0 - distance.astype(jnp.float32) / (modulus // 16), 0.0)

def gradient_terms(windowed):
    line_count = windowed.shape[1]
    spectrum = forward_split(windowed.reshape(2, line_count, A1, A2), A1, A2, True).reshape(2, line_count, A1 * A2)
    following = jnp.roll(spectrum, -1, axis=2)
    cross_terms = spectrum[0] * following[1] - spectrum[1] * following[0]
    energy = spectrum[0] * spectrum[0] + spectrum[1] * spectrum[1]
    return (cross_terms.reshape(line_count, MAZ, -1).sum(axis=2), energy.reshape(line_count, MAZ, -1).sum(axis=2))

def reference(echoes, scale_rate, migration, range_phase, azimuth_rate, bright_columns, line_block, line_center):
    block_lines = 64
    block_count = AZ // block_lines

    def range_step(operands):
        return range_lines(operands[0], operands[1], operands[2], range_phase)
    compressed = lax.map(range_step, (echoes.reshape(2, block_count, block_lines, RG).transpose(1, 0, 2, 3), scale_rate.reshape(block_count, block_lines), migration.reshape(block_count, block_lines)))
    compressed = compressed.transpose(1, 0, 2, 3).reshape(2, AZ, RG)
    column_block = 128
    column_count = RG // column_block

    def azimuth_step(operands):
        return azimuth_columns(operands[0], operands[1])
    focused = lax.map(azimuth_step, (compressed.reshape(2, AZ, column_count, column_block).transpose(2, 0, 1, 3), azimuth_rate.reshape(column_count, column_block)))
    focused_image = focused.transpose(1, 2, 0, 3).reshape(2, AZ, RG)
    group_width = RG // N_FORM
    global_cols = (bright_columns + (jnp.arange(N_FORM, dtype=jnp.int32) * group_width)[:, None]).reshape(-1).astype(jnp.int32)
    line_data = jnp.transpose(jnp.take(focused_image, global_cols, axis=2), (0, 2, 1))
    windowed = (line_data.astype(jnp.float32) * taper(line_center.reshape(-1), AZ)[None]).astype(jnp.bfloat16)
    cross_terms, energy = gradient_terms(windowed)
    onehot = (line_block.reshape(-1)[:, None] == jnp.arange(NBLK, dtype=jnp.int32)[None, :]).astype(jnp.float32)
    block_maps = jnp.einsum('lb,slm->sbm', onehot, jnp.stack([cross_terms, energy]), precision=lax.Precision.HIGHEST)
    phase_map = block_maps[0] / (block_maps[1] + EPSILON)
    return (focused_image, phase_map)
```

```python
import math

import jax
import jax.numpy as jnp
import numpy as np
from jax import lax
from jax.sharding import PartitionSpec as P

A1 = 64
A2 = 128
R1 = 256
R2 = 128
NBLK = 256
MAZ = 256


TWO_PI = 2.0 * math.pi
EPSILON = 1e-06


def section_table(factor, signum):
    indices = np.arange(factor)
    products = indices[:, None] * indices[None, :] % factor
    angles = signum * TWO_PI / factor * products
    scaling = 1.0 / math.sqrt(factor)
    cosine = np.cos(angles) * scaling
    sine_part = np.sin(angles) * scaling
    upper_rows = np.stack([cosine, -sine_part], axis=1)
    lower_rows = np.stack([sine_part, cosine], axis=1)
    return np.stack([upper_rows, lower_rows], axis=0).astype(jnp.bfloat16)


def twiddle_pair(outer_size, inner_size, modulus, signum):
    first_idx = np.arange(outer_size)[:, None]
    second_idx = np.arange(inner_size)[None, :]
    angles = signum * TWO_PI / modulus * (first_idx * second_idx % modulus)
    return (np.cos(angles).astype(np.float32), np.sin(angles).astype(np.float32))


def cos_sin(angles):
    turns = jnp.round(angles * (1.0 / TWO_PI))
    rest = (angles - turns * 6.28125) - turns * (TWO_PI - 6.28125)
    quarter = rest * 0.5
    square = quarter * quarter
    sine = quarter * (
        1.0
        + square
        * (-1.0 / 6 + square * (1.0 / 120 + square * (-1.0 / 5040 + square * (1.0 / 362880 - square / 39916800))))
    )
    cosine = 1.0 + square * (
        -0.5
        + square
        * (1.0 / 24 + square * (-1.0 / 720 + square * (1.0 / 40320 + square * (-1.0 / 3628800 + square / 479001600))))
    )
    return (1.0 - 2.0 * sine * sine, 2.0 * sine * cosine)


def rotate(real_part, imag_part, cosine, sine_part):
    return (real_part * cosine - imag_part * sine_part, real_part * sine_part + imag_part * cosine)


def rounded(pair):
    return jnp.stack([pair[0], pair[1]]).astype(jnp.bfloat16)


def mix(pattern, matrix, values):
    return jnp.einsum(pattern, matrix, values, preferred_element_type=jnp.float32)


def forward_split(values, outer_size, inner_size):
    modulus = outer_size * inner_size
    first_section = mix("akcn,clnq->alkq", section_table(outer_size, -1.0), values)
    cosine, sine_part = twiddle_pair(outer_size, inner_size, modulus, -1.0)
    twisted = rounded(rotate(first_section[0], first_section[1], cosine[None], sine_part[None]))
    return mix("apcq,clkq->alpk", section_table(inner_size, -1.0), twisted)


def range_lines(echo_part, rate_part, shift_part, range_phase):
    line_count = echo_part.shape[1]
    length = R1 * R2
    offsets = (jnp.arange(length, dtype=jnp.int32) - length // 2).astype(jnp.float32) / length
    angles = rate_part[:, None] * (offsets * offsets)[None, :]
    chirped = rounded(
        rotate(
            echo_part[0].astype(jnp.float32),
            echo_part[1].astype(jnp.float32),
            *cos_sin(angles),
        )
    )
    first_section = mix(
        "akcn,clnq->aklq", section_table(R1, -1.0), chirped.reshape(2, line_count, R1, R2)
    )
    cosine, sine_part = twiddle_pair(R1, R2, length, -1.0)
    twisted = rounded(
        rotate(first_section[0], first_section[1], cosine[:, None, :], sine_part[:, None, :])
    )
    spectrum = mix("apcq,cklq->klap", section_table(R2, -1.0), twisted)
    freq_bins = (
        jnp.arange(R1, dtype=jnp.int32)[:, None] + R1 * jnp.arange(R2, dtype=jnp.int32)[None, :]
    )
    signed = jnp.where(freq_bins >= length // 2, freq_bins - length, freq_bins).astype(jnp.float32)
    phases = (
        range_phase.reshape(R2, R1).T[:, None, :]
        + TWO_PI / length * signed[:, None, :] * shift_part[None, :, None]
    )
    matched = rounded(rotate(spectrum[:, :, 0], spectrum[:, :, 1], *cos_sin(-phases)))
    back_section = mix("aqcp,cklp->klaq", section_table(R2, 1.0), matched)
    cosine, sine_part = twiddle_pair(R1, R2, length, 1.0)
    twisted = rounded(
        rotate(
            back_section[:, :, 0], back_section[:, :, 1], cosine[:, None, :], sine_part[:, None, :]
        )
    )
    return mix("anck,cklq->anlq", section_table(R1, 1.0), twisted).astype(jnp.bfloat16)


def azimuth_columns(columns, rate_part):
    col_width = columns.shape[2]
    modulus = A1 * A2
    shaped = columns.reshape(2, A1, A2, col_width)
    first_section = mix("akcm,cmqr->akqr", section_table(A1, -1.0), shaped)
    cosine, sine_part = twiddle_pair(A1, A2, modulus, -1.0)
    twisted = rounded(
        rotate(first_section[0], first_section[1], cosine[:, :, None], sine_part[:, :, None])
    )
    doppler = mix("apcq,ckqr->apkr", section_table(A2, -1.0), twisted)
    freq_bins = (
        A1 * jnp.arange(A2, dtype=jnp.int32)[:, None] + jnp.arange(A1, dtype=jnp.int32)[None, :]
    )
    signed = (
        jnp.where(freq_bins >= modulus // 2, freq_bins - modulus, freq_bins).astype(jnp.float32)
        / modulus
    )
    angles = (signed * signed)[:, :, None] * rate_part[None, None, :]
    history = rounded(rotate(doppler[0], doppler[1], *cos_sin(-angles)))
    first_back = mix("amcq,cqkr->amkr", section_table(A2, 1.0), history)
    cosine, sine_part = twiddle_pair(A1, A2, modulus, 1.0)
    twisted = rounded(
        rotate(first_back[0], first_back[1], cosine.T[:, :, None], sine_part.T[:, :, None])
    )
    restored = mix("anck,cmkr->anmr", section_table(A1, 1.0), twisted)
    return restored.reshape(2, modulus, col_width).astype(jnp.bfloat16)


def taper(centers, modulus):
    positions = jnp.arange(modulus, dtype=jnp.int32)
    offsets = (positions - centers[..., None]) % modulus
    distance = jnp.minimum(offsets, modulus - offsets)
    return jnp.maximum(1.0 - distance.astype(jnp.float32) / (modulus // 16), 0.0)


def gradient_terms(windowed):
    line_count = windowed.shape[1]
    spectrum = forward_split(windowed.reshape(2, line_count, A1, A2), A1, A2).reshape(
        2, line_count, A1 * A2
    )
    following = jnp.roll(spectrum, -1, axis=2)
    cross_terms = spectrum[0] * following[1] - spectrum[1] * following[0]
    energy = spectrum[0] * spectrum[0] + spectrum[1] * spectrum[1]
    return (
        cross_terms.reshape(line_count, MAZ, -1).sum(axis=2),
        energy.reshape(line_count, MAZ, -1).sum(axis=2),
    )


def on_device(
    echoes,
    scale_rate,
    migration,
    range_phase,
    azimuth_rate,
    bright_columns,
    line_block,
    line_center,
):
    compressed = range_lines(echoes, scale_rate, migration, range_phase)
    arrived = lax.all_to_all(
        compressed, ("form", "focus"), split_axis=1, concat_axis=1, tiled=True
    )
    col_width = arrived.shape[-1]
    columns = arrived.reshape(2, -1, col_width)
    focused_image = azimuth_columns(columns, azimuth_rate)
    modulus = columns.shape[1]
    focus_index = lax.axis_index("focus")
    local_cols = bright_columns[0] - focus_index * col_width
    column_ids = jnp.arange(col_width, dtype=jnp.int32)
    centers = line_center[0]
    blocks = line_block[0, :, 0]
    select = (local_cols[:, None] == column_ids[None, :]).astype(jnp.bfloat16)
    picked = jnp.einsum("car,lr->cla", focused_image, select, preferred_element_type=jnp.float32)
    windowed = (picked * taper(centers, modulus)[None]).astype(jnp.bfloat16)
    cross_terms, energy = gradient_terms(windowed)
    onehot = (blocks[:, None] == jnp.arange(NBLK, dtype=jnp.int32)[None, :]).astype(jnp.float32)
    partial_maps = jnp.einsum(
        "lb,slm->bsm", onehot, jnp.stack([cross_terms, energy]), precision=lax.Precision.HIGHEST
    )
    own_rows = lax.all_to_all(
        partial_maps, ("form", "focus"), split_axis=0, concat_axis=0, tiled=True
    ).sum(axis=0)
    phase_map = (own_rows[0] / (own_rows[1] + EPSILON))[None]
    return (focused_image, phase_map)


def solution(mesh):
    in_specs = (
        P(None, ("form", "focus"), None),
        P(("form", "focus")),
        P(("form", "focus")),
        P(),
        P(("form", "focus")),
        P("form", None),
        P("form", None, None),
        P("form", None),
    )
    out_specs = (P(None, None, ("form", "focus")), P(("form", "focus"), None))
    return jax.shard_map(
        on_device, mesh=mesh, in_specs=in_specs, out_specs=out_specs, check_vma=False
    )
```

```python
import functools
import math

import jax
import jax.numpy as jnp
import ml_dtypes
import numpy as np
from jax import lax
from jax.experimental import pallas as pl
from jax.experimental.pallas import tpu as pltpu
from jax.sharding import PartitionSpec as P

R1 = 256
R2 = 128
NBLK = 256
AZ = 8192
CHUNKS = 4
LINES = 8
MESH = pl.DeviceIdType.MESH
F32 = jnp.float32
BF16 = jnp.bfloat16

TWO_PI = 2.0 * math.pi
EPSILON = 1e-06


def real_blocks(values):
    upper = np.stack([values.real, -values.imag], axis=-2)
    lower = np.stack([values.imag, values.real], axis=-2)
    return np.stack([upper, lower], axis=-4)


def unit(turns):
    return np.exp(2j * np.pi * turns)


def range_tables():
    k = np.arange(R1)
    n = np.arange(R2)
    wide = np.outer(k, k) % R1 / R1
    narrow = np.outer(n, n) % R2 / R2
    first = real_blocks(unit(-wide) / 16).reshape(2 * R1, 2 * R1)
    last = real_blocks(unit(wide) / 16).reshape(2 * R1, 2 * R1)
    inner = real_blocks(unit(-narrow) / math.sqrt(R2)).reshape(2 * R2, 2 * R2).T
    outer = real_blocks(unit(narrow) / math.sqrt(R2)).reshape(2 * R2, 2 * R2).T
    twist = unit(np.outer(k, n) / (R1 * R2))
    length = R1 * R2
    offsets = (k[:, None] * R2 + n[None, :] - length // 2) / length
    bins = k[:, None] + R1 * n[None, :]
    signed = np.where(bins >= length // 2, bins - length, bins) / length
    planes = np.stack([twist.real, twist.imag, offsets * offsets / TWO_PI, signed])
    swap = np.eye(256).reshape(LINES, 2, 16, 256).transpose(2, 1, 0, 3).reshape(256, 256)
    half = [t.astype(ml_dtypes.bfloat16) for t in (first, inner, outer, last, swap)]
    return half + [planes.astype(np.float32)]


def spread(blocks):
    full = np.einsum("...atcf,lm->...talfcm", blocks, np.eye(LINES))
    return full.reshape(*blocks.shape[:-4], 256, 256).astype(ml_dtypes.bfloat16)


def azimuth_tables():
    i = np.arange(16)
    near = np.outer(i, i) / 16
    shift = (i[:, None] * i[None, :] / 256)
    first = spread(real_blocks(unit(-near[None] - shift[:, :, None]) / 4))
    second = spread(real_blocks(unit(-near) / 4))
    third = spread(real_blocks(unit(near[None] + shift[:, :, None]) / 4))
    fourth = spread(real_blocks(unit(near) / 4))
    ks, l, m = np.arange(256)[:, None, None], np.arange(32), np.arange(32)
    turns = l[None, None, :] * ks / AZ + m[None, :, None] * l[None, None, :] / 32
    fwd = real_blocks(unit(-turns) / math.sqrt(32)).reshape(256, 2, 32, 2, 4, 8)
    fwd = fwd.transpose(0, 1, 2, 4, 3, 5).reshape(256, 64, 64)
    back = real_blocks(unit(turns.transpose(0, 2, 1)) / math.sqrt(32)).reshape(256, 2, 4, 8, 2, 32)
    back = back.transpose(0, 2, 1, 3, 4, 5).reshape(256, 64, 64)
    middle = np.concatenate([fwd, back], axis=2).astype(ml_dtypes.bfloat16)
    return first, second, middle, third, fourth


def cos_sin(turns):
    rest = turns - jnp.round(turns)
    z = rest * rest
    sine = rest * (6.28316395 + z * (-10.3342826 + z * (5.08377413 - 1.1092177 * z)))
    cosine = 0.99999995 + z * (-4.93479283 + z * (4.05841135 + z * (-1.33187657 + 0.21968961 * z)))
    return 1.0 - 0.5 * (sine * sine), sine * cosine


def dot(a, b):
    return jnp.dot(a, b, preferred_element_type=F32)


def range_kernel(
    x_hbm, rate, shift, rp, first, inner, outer, last, swap, planes, out_hbm,
    xbuf, rows, send, in_sem, send_sem, recv_sem, own_sem, *, talk=True,
):
    loads = [
        pltpu.make_async_copy(x_hbm.at[:, pl.ds(LINES * c, LINES)], xbuf.at[c], in_sem.at[c])
        for c in range(CHUNKS)
    ]
    for load in loads:
        load.start()
    if talk:
        form = lax.axis_index("form")
        focus = lax.axis_index("focus")
        me = form * 4 + focus

    def chunk(c, _):
        pltpu.make_async_copy(x_hbm.at[:, pl.ds(LINES * c, LINES)], xbuf.at[c], in_sem.at[c]).wait()

        def two_lines(p, _):
            parts = []
            for i in range(2):
                l = 2 * p + i
                cosine, sine = cos_sin(rate[LINES * c + l] * planes[2])
                re = xbuf[c, 0, l].astype(F32)
                im = xbuf[c, 1, l].astype(F32)
                parts.append(
                    jnp.concatenate(
                        [
                            (re * cosine - im * sine).astype(BF16),
                            (re * sine + im * cosine).astype(BF16),
                        ],
                        axis=0,
                    )
                )
            u = dot(first[...], jnp.concatenate(parts, axis=1))
            parts = []
            for i in range(2):
                lanes = slice(R2 * i, R2 * i + R2)
                re, im = u[:R1, lanes], u[R1:, lanes]
                cosine, sine = planes[0], planes[1]
                twisted = jnp.concatenate(
                    [
                        (re * cosine + im * sine).astype(BF16),
                        (im * cosine - re * sine).astype(BF16),
                    ],
                    axis=1,
                )
                spectrum = dot(twisted, inner[...])
                re, im = spectrum[:, :R2], spectrum[:, R2:]
                cosine, sine = cos_sin(rp[...] + shift[LINES * c + 2 * p + i] * planes[3])
                matched = jnp.concatenate(
                    [
                        (re * cosine + im * sine).astype(BF16),
                        (im * cosine - re * sine).astype(BF16),
                    ],
                    axis=1,
                )
                w = dot(matched, outer[...])
                re, im = w[:, :R2], w[:, R2:]
                cosine, sine = planes[0], planes[1]
                parts.append(
                    jnp.concatenate(
                        [
                            (re * cosine - im * sine).astype(BF16),
                            (re * sine + im * cosine).astype(BF16),
                        ],
                        axis=0,
                    )
                )
            done = dot(last[...], jnp.concatenate(parts, axis=1)).astype(BF16)
            for i in range(2):
                for a in range(2):
                    rows[2 * p + i, a] = done[R1 * a : R1 * a + R1, R2 * i : R2 * i + R2]
            return 0

        lax.fori_loop(0, LINES // 2, two_lines, 0)

        def swapped(t, _):
            cut = [
                rows[:, :, pl.ds(pl.multiple_of(32 * t + 16 * i, 16), 16)].reshape(256, R2)
                for i in range(2)
            ]
            out = dot(swap[...], jnp.concatenate(cut, axis=1)).astype(BF16)
            for i in range(2):
                send[c, pl.ds(32 * t + 16 * i, 16)] = out[:, R2 * i : R2 * i + R2].reshape(16, 16, R2)
            return 0

        lax.fori_loop(0, 8, swapped, 0, unroll=2)
        if not talk:
            return 0
        pltpu.make_async_copy(send.at[c, me], out_hbm.at[c, me], own_sem).start()

        def sends(j, _):
            dy = lax.rem(j, 4)
            other = focus + dy
            other = jnp.where(other >= 4, other - 4, other)
            base = form + lax.div(j, 4)
            for dz in (4, 3, 5, 2, 6, 1, 7, 0):
                group = base + 8 * dz
                group = jnp.where(group >= 64, group - 64, group)

                def go():
                    pltpu.make_async_remote_copy(
                        src_ref=send.at[c, group * 4 + other],
                        dst_ref=out_hbm.at[c, me],
                        send_sem=send_sem,
                        recv_sem=recv_sem,
                        device_id=(group, other),
                        device_id_type=MESH,
                    ).start()

                if dz == 0:
                    pl.when(j > 0)(go)
                else:
                    go()
            return 0

        lax.fori_loop(0, 32, sends, 0)
        return 0

    lax.fori_loop(0, CHUNKS, chunk, 0)
    if not talk:
        copy = pltpu.make_async_copy(send, out_hbm, own_sem)
        copy.start()
        copy.wait()
        return
    pltpu.make_async_copy(send.at[:, 0], out_hbm.at[:, 0], own_sem).wait()
    pltpu.make_async_copy(send.at[:, pl.ds(0, 255)], out_hbm.at[:, pl.ds(0, 255)], send_sem).wait()
    pltpu.make_async_copy(send.at[:, pl.ds(0, 255)], out_hbm.at[:, pl.ds(0, 255)], recv_sem).wait()


def corner_turned(echoes, rate, shift, range_phase, talk=True):
    x = echoes.reshape(2, CHUNKS * LINES, R1, R2)
    rp = range_phase.reshape(R2, R1).T * (1.0 / TWO_PI)
    vmem = pl.BlockSpec(memory_space=pltpu.VMEM)
    smem = pl.BlockSpec(memory_space=pltpu.SMEM)
    hbm = pl.BlockSpec(memory_space=pl.ANY)
    return pl.pallas_call(
        functools.partial(range_kernel, talk=talk),
        out_shape=jax.ShapeDtypeStruct((CHUNKS, 256, 2 * LINES, R2), BF16),
        in_specs=[hbm, smem, smem] + [vmem] * 7,
        out_specs=hbm,
        scratch_shapes=[
            pltpu.VMEM((CHUNKS, 2, LINES, R1, R2), BF16),
            pltpu.VMEM((LINES, 2, R1, R2), BF16),
            pltpu.VMEM((CHUNKS, 256, 2 * LINES, R2), BF16),
            pltpu.SemaphoreType.DMA((CHUNKS,)),
            pltpu.SemaphoreType.DMA,
            pltpu.SemaphoreType.DMA,
            pltpu.SemaphoreType.DMA,
        ],
        compiler_params=pltpu.CompilerParams(has_side_effects=True, vmem_limit_bytes=48 * 2**20),
        cost_estimate=pl.CostEstimate(flops=7 * 10**9, bytes_accessed=10**7, transcendentals=0),
        name="range_lines",
    )(x, rate, shift, rp, *[jnp.asarray(t) for t in range_tables()])


def azimuth_kernel(
    r_hbm, first_hbm, middle_hbm, third_hbm, second, fourth, rate, sel, centers, img_hbm, terms,
    r, y, z, first, middle, third, img, sems, tab_sems, out_sem,
):
    loads = [
        pltpu.make_async_copy(r_hbm.at[pl.ds(2 * h, 2)], r.at[pl.ds(2 * h, 2)], sems.at[h])
        for h in range(2)
    ]
    tables = [
        pltpu.make_async_copy(a, b, tab_sems.at[i])
        for i, (a, b) in enumerate([(first_hbm, first), (middle_hbm, middle), (third_hbm, third)])
    ]
    tables[0].start()
    loads[0].start()
    loads[1].start()
    tables[1].start()
    tables[2].start()

    def pair_of(ref, h, *index):
        return jnp.concatenate([ref[(2 * h + i, *index)].reshape(256, R2) for i in range(2)], axis=1)

    def forward(wait):
        for h in range(2):
            if wait:
                if h == 0:
                    tables[0].wait()
                loads[h].wait()

            def one(s, _):
                out = dot(first[s], pair_of(r, h, slice(None), s)).astype(BF16)
                for i in range(2):
                    y[2 * h + i, :, s] = out[:, R2 * i : R2 * i + R2].reshape(16, 16, R2)
                return 0

            lax.fori_loop(0, 16, one, 0, unroll=4)
        for h in range(2):

            def two(k, _):
                out = dot(second[...], pair_of(y, h, k)).astype(BF16)
                for i in range(2):
                    z[:, k, 2 * h + i] = out[:, R2 * i : R2 * i + R2].reshape(16, 16, R2)
                return 0

            lax.fori_loop(0, 16, two, 0, unroll=4)

    nothing = jnp.zeros((64, R2), BF16)

    def spectrum(k):
        k2, k1 = lax.div(k, 16), lax.rem(k, 16)
        v = dot(middle[k], jnp.concatenate([z[k2, k1].reshape(64, R2), nothing], axis=0))
        return v[:32], v[32:]

    forward(True)
    tables[1].wait()
    m = lax.broadcasted_iota(jnp.int32, (32, R2), 0)
    m = jnp.where(m >= 16, m - 32, m).astype(F32) * (1.0 / 32)
    cycles = rate[...] * (1.0 / TWO_PI)

    def filtered(k, _):
        re, im = spectrum(k)
        f = m + k.astype(F32) * (1.0 / AZ)
        cosine, sine = cos_sin(f * f * cycles)
        history = jnp.concatenate(
            [
                nothing,
                (re * cosine + im * sine).astype(BF16),
                (im * cosine - re * sine).astype(BF16),
            ],
            axis=0,
        )
        z[lax.div(k, 16), lax.rem(k, 16)] = dot(middle[k], history).astype(BF16).reshape(4, 16, R2)
        return 0

    lax.fori_loop(0, 256, filtered, 0, unroll=8)
    tables[2].wait()
    for h in range(2):

        def three(k, _):
            out = jnp.concatenate([z[:, k, 2 * h + i].reshape(256, R2) for i in range(2)], axis=1)
            out = dot(third[k], out).astype(BF16)
            for i in range(2):
                y[2 * h + i, :, k] = out[:, R2 * i : R2 * i + R2].reshape(16, 16, R2)
            return 0

        lax.fori_loop(0, 16, three, 0, unroll=4)
    for h in range(2):

        def four(s, _):
            out = dot(fourth[...], pair_of(y, h, s))
            out = out.reshape(16, 2, LINES, 2 * R2)
            out = jnp.concatenate([out[..., :R2], out[..., R2:]], axis=2).astype(BF16)
            for a in range(2):
                img[a, :, s, 16 * h : 16 * h + 16] = out[:, a]
            return 0

        lax.fori_loop(0, 16, four, 0, unroll=4)
    image_out = pltpu.make_async_copy(img, img_hbm, out_sem)
    image_out.start()

    line = lax.broadcasted_iota(jnp.int32, (256, R2), 0)

    def windowed(t, _):
        hi, lo = lax.div(t, 2), lax.rem(t, 2) * 8
        away = jnp.bitwise_and(line + 256 * t - centers[...], AZ - 1)
        away = jnp.minimum(away, AZ - away).astype(F32)
        window = jnp.maximum(1.0 - away * (16.0 / AZ), 0.0)
        parts = [
            (dot(img[a, hi, pl.ds(lo, 8)].reshape(256, R2), sel[...]) * window).reshape(8, 4, 1, LINES, R2)
            for a in range(2)
        ]
        both = jnp.concatenate(parts, axis=2).astype(BF16)
        for c in range(CHUNKS):
            r[c, hi, pl.ds(lo, 8)] = both[:, c].reshape(8, 16, R2)
        return 0

    lax.fori_loop(0, 32, windowed, 0, unroll=2)
    forward(False)

    first_re, first_im = spectrum(0)
    end_re, end_im = pltpu.roll(first_re, 31, 0), pltpu.roll(first_im, 31, 0)

    def group(g, carry):
        re, im = carry
        cross = jnp.zeros((32, R2), F32)
        energy = jnp.zeros((32, R2), F32)
        for i in range(32):
            k = g * 32 + i + 1
            if i < 31:
                next_re, next_im = spectrum(k)
            else:
                next_re, next_im = spectrum(lax.rem(k, 256))
                next_re = jnp.where(g == 7, end_re, next_re)
                next_im = jnp.where(g == 7, end_im, next_im)
            cross += re * next_im - im * next_re
            energy += re * re + im * im
            re, im = next_re, next_im
        terms[0, g] = cross
        terms[1, g] = energy
        return re, im

    lax.fori_loop(0, 8, group, (first_re, first_im))
    image_out.wait()


def focused(arrived, rate, sel, centers):
    vmem = pl.BlockSpec(memory_space=pltpu.VMEM)
    hbm = pl.BlockSpec(memory_space=pl.ANY)
    first, second, middle, third, fourth = [jnp.asarray(t) for t in azimuth_tables()]
    image, terms = pl.pallas_call(
        azimuth_kernel,
        out_shape=(
            jax.ShapeDtypeStruct((2, 16, 16, 32, R2), BF16),
            jax.ShapeDtypeStruct((2, 8, 32, R2), F32),
        ),
        in_specs=[hbm] * 4 + [vmem] * 5,
        out_specs=(hbm, vmem),
        scratch_shapes=[
            pltpu.VMEM((4, 16, 16, 16, R2), BF16),
            pltpu.VMEM((4, 16, 16, 16, R2), BF16),
            pltpu.VMEM((16, 16, 4, 16, R2), BF16),
            pltpu.VMEM((16, 256, 256), BF16),
            pltpu.VMEM((256, 64, 128), BF16),
            pltpu.VMEM((16, 256, 256), BF16),
            pltpu.VMEM((2, 16, 16, 32, R2), BF16),
            pltpu.SemaphoreType.DMA((2,)),
            pltpu.SemaphoreType.DMA((3,)),
            pltpu.SemaphoreType.DMA,
        ],
        compiler_params=pltpu.CompilerParams(vmem_limit_bytes=56 * 2**20),
        cost_estimate=pl.CostEstimate(flops=15 * 10**9, bytes_accessed=2 * 10**7, transcendentals=0),
        name="azimuth_columns",
    )(arrived.reshape(4, 16, 16, 16, R2), first, middle, third, second, fourth, rate[None], sel, centers)
    return image.reshape(2, AZ, R2), terms


def on_device(
    echoes,
    scale_rate,
    migration,
    range_phase,
    azimuth_rate,
    bright_columns,
    line_block,
    line_center,
):
    arrived = corner_turned(echoes, scale_rate, migration, range_phase)
    local_cols = bright_columns[0] - lax.axis_index("focus") * R2
    spare = (0, R2 - local_cols.shape[0])
    local_cols = jnp.pad(local_cols, spare, constant_values=-1)
    sel = (jnp.arange(R2, dtype=jnp.int32)[:, None] == local_cols[None, :]).astype(BF16)
    centers = jnp.pad(line_center[0], spare)[None]
    blocks = jnp.pad(line_block[0, :, 0], spare, constant_values=-1)
    focused_image, terms = focused(arrived, azimuth_rate, sel, centers)
    onehot = (jnp.arange(NBLK, dtype=jnp.int32)[:, None] == blocks[None, :]).astype(F32)
    partial_maps = jnp.einsum(
        "bl,sgml->bsgm", onehot, terms, precision=lax.Precision.HIGHEST
    )
    own_rows = lax.all_to_all(
        partial_maps.reshape(NBLK, 2, 256), ("form", "focus"), split_axis=0, concat_axis=0, tiled=True
    ).sum(axis=0)
    own_map = own_rows[0] / (own_rows[1] + EPSILON)
    phase_map = own_map.reshape(8, 32).T.reshape(1, 256)
    return (focused_image, phase_map)


def solution(mesh):
    in_specs = (
        P(None, ("form", "focus"), None),
        P(("form", "focus")),
        P(("form", "focus")),
        P(),
        P(("form", "focus")),
        P("form", None),
        P("form", None, None),
        P("form", None),
    )
    out_specs = (P(None, None, ("form", "focus")), P(("form", "focus"), None))
    return jax.shard_map(
        on_device, mesh=mesh, in_specs=in_specs, out_specs=out_specs, check_vma=False
    )
```

```python
import functools
import math

import jax
import jax.numpy as jnp
import ml_dtypes
import numpy as np
from jax import lax
from jax.experimental import pallas as pl
from jax.experimental.pallas import tpu as pltpu
from jax.sharding import PartitionSpec as P

R1 = 256
R2 = 128
NBLK = 256
AZ = 8192
CHUNKS = 4
LISTED = 32
LINES = 8
MESH = pl.DeviceIdType.MESH
F32 = jnp.float32
BF16 = jnp.bfloat16

TWO_PI = 2.0 * math.pi
EPSILON = 1e-06


def real_blocks(values):
    upper = np.stack([values.real, -values.imag], axis=-2)
    lower = np.stack([values.imag, values.real], axis=-2)
    return np.stack([upper, lower], axis=-4)


def unit(turns):
    return np.exp(2j * np.pi * turns)


def range_tables():
    k = np.arange(R1)
    n = np.arange(R2)
    wide = np.outer(k, k) % R1 / R1
    narrow = np.outer(n, n) % R2 / R2
    first = real_blocks(unit(-wide) / 16).reshape(2 * R1, 2 * R1)
    last = real_blocks(unit(wide) / 16).reshape(2 * R1, 2 * R1)
    inner = real_blocks(unit(-narrow) / math.sqrt(R2)).reshape(2 * R2, 2 * R2).T
    outer = real_blocks(unit(narrow) / math.sqrt(R2)).reshape(2 * R2, 2 * R2).T
    twist = unit(np.outer(k, n) / (R1 * R2))
    length = R1 * R2
    offsets = (k[:, None] * R2 + n[None, :] - length // 2) / length
    bins = k[:, None] + R1 * n[None, :]
    signed = np.where(bins >= length // 2, bins - length, bins) / length
    planes = np.stack([twist.real, twist.imag, offsets * offsets / TWO_PI, signed])
    swap = np.eye(256).reshape(LINES, 2, 16, 256).transpose(2, 1, 0, 3).reshape(256, 256)
    cross = np.eye(256).reshape(16, 16, 256).transpose(1, 0, 2).reshape(256, 256)
    half = [t.astype(ml_dtypes.bfloat16) for t in (first, inner, outer, last, swap, cross)]
    return half + [planes.astype(np.float32)]


def azimuth_tables():
    i = np.arange(16)
    near = np.outer(i, i) / 16
    shift = np.outer(i, i) / 256
    l8, m = np.arange(LINES), np.arange(32)
    eye = np.eye(LINES)

    def widened(turns):
        blocks = real_blocks(np.moveaxis(unit(turns) / 4, -1, 0))
        full = np.einsum("l...atcf,lm->...talfcm", blocks, eye)
        return full.reshape(*full.shape[:-6], 256, 256)

    same = np.zeros(LINES)
    lines = LINES * np.arange(CHUNKS)[:, None] + l8
    first = widened(-(near[None] + shift[:, :, None])[..., None] - same)
    second = widened(-near[None, :, :, None] - (i[:, None] * lines[:, None, :] / 512)[:, :, None, :])
    part = (lines[None] * i[:, None, None] / AZ)[:, None] + (lines * m[:, None, None] / 32)[None]
    wide = real_blocks((unit(-part) / math.sqrt(32)).reshape(16, 32, 32)).reshape(16, 2, 32, 2, CHUNKS, LINES)
    third = np.einsum("kamchl,xy->kxamyhcl", wide, np.eye(4)).reshape(16, 256, 256)
    wide = real_blocks((unit(part) / math.sqrt(32)).transpose(0, 2, 3, 1).reshape(16, 32, 32))
    wide = wide.reshape(16, 2, CHUNKS, LINES, 2, 32)
    fourth = np.einsum("kahlcm,xy->kxhalycm", wide, np.eye(4)).reshape(16, 256, 256)
    fifth = widened(near[None, :, :, None] + (i[:, None] * lines[:, None, :] / 512)[:, None, :, :])
    sixth = widened((near[None] + shift[:, None, :])[..., None] + same)
    return [t.astype(ml_dtypes.bfloat16) for t in (first, second, third, fourth, fifth, sixth)]


def cos_sin(turns):
    rest = turns - jnp.round(turns)
    z = rest * rest
    sine = rest * (6.28316395 + z * (-10.3342826 + z * (5.08377413 - 1.1092177 * z)))
    cosine = 0.99999995 + z * (-4.93479283 + z * (4.05841135 + z * (-1.33187657 + 0.21968961 * z)))
    return 1.0 - 0.5 * (sine * sine), sine * cosine


def dot(a, b):
    return jnp.dot(a, b, preferred_element_type=F32)


def range_kernel(
    x_hbm, rate, shift, phase, *args, talk=True,
):
    sources, out_hbm, tables = args[:7], args[7], args[8:15]
    raw, xbuf, rp, rows, send, in_sem, tab_sem, send_sem, recv_sem, own_sem = args[15:]
    first, inner, outer, last, swap, cross, planes = tables
    loads = [
        pltpu.make_async_copy(x_hbm.at[:, pl.ds(16 * h, 16)], raw.at[h], in_sem.at[h]) for h in range(2)
    ]
    copies = [pltpu.make_async_copy(a, b, tab_sem.at[i]) for i, (a, b) in enumerate(zip(sources, tables))]
    loads[0].start()
    for i in (5, 6, 0, 1, 2, 3, 4):
        copies[i].start()
    loads[1].start()
    rp[...] = phase[...].T * (1.0 / TWO_PI)
    copies[5].wait()
    if talk:
        form = lax.axis_index("form")
        focus = lax.axis_index("focus")
        me = form * 4 + focus
        barrier = pltpu.get_barrier_semaphore()

        def greet(j, _):
            for d in range(8):
                group = form + j + 8 * d
                group = jnp.where(group >= 64, group - 64, group)
                for dy in range(4):
                    other = focus + dy
                    other = jnp.where(other >= 4, other - 4, other)

                    def hello():
                        pl.semaphore_signal(
                            barrier, inc=1, device_id=(group, other), device_id_type=MESH
                        )

                    if d == 0 and dy == 0:
                        pl.when(j > 0)(hello)
                    else:
                        hello()
            return 0

        lax.fori_loop(0, 8, greet, 0)

    def chunk(c, _):
        h = lax.div(c, 2)

        @pl.when(lax.rem(c, 2) == 0)
        def _():
            pltpu.make_async_copy(x_hbm.at[:, pl.ds(16 * h, 16)], raw.at[h], in_sem.at[h]).wait()

            def unfold(t, _):
                cut = [
                    jnp.concatenate(
                        [
                            raw[h, a, :, pl.ds(pl.multiple_of(2048 * t + R2 * i, R2), R2)]
                            for i in range(16)
                        ],
                        axis=0,
                    )
                    for a in range(2)
                ]
                out = dot(cross[...], jnp.concatenate(cut, axis=1)).astype(BF16)
                for a in range(2):
                    xbuf[a, :, pl.ds(pl.multiple_of(16 * t, 16), 16)] = out[
                        :, R2 * a : R2 * a + R2
                    ].reshape(16, 16, R2)
                return 0

            lax.fori_loop(0, 16, unfold, 0, unroll=4)

        @pl.when(c == 0)
        def _():
            for i in (6, 0, 1, 2, 3, 4):
                copies[i].wait()

        half = LINES * lax.rem(c, 2)

        def two_lines(p, _):
            parts = []
            for i in range(2):
                l = 2 * p + i
                cosine, sine = cos_sin(rate[LINES * c + l] * planes[2])
                re = xbuf[0, half + l].astype(F32)
                im = xbuf[1, half + l].astype(F32)
                parts.append(
                    jnp.concatenate(
                        [
                            (re * cosine - im * sine).astype(BF16),
                            (re * sine + im * cosine).astype(BF16),
                        ],
                        axis=0,
                    )
                )
            u = dot(first[...], jnp.concatenate(parts, axis=1))
            parts = []
            for i in range(2):
                lanes = slice(R2 * i, R2 * i + R2)
                re, im = u[:R1, lanes], u[R1:, lanes]
                cosine, sine = planes[0], planes[1]
                twisted = jnp.concatenate(
                    [
                        (re * cosine + im * sine).astype(BF16),
                        (im * cosine - re * sine).astype(BF16),
                    ],
                    axis=1,
                )
                spectrum = dot(twisted, inner[...])
                re, im = spectrum[:, :R2], spectrum[:, R2:]
                cosine, sine = cos_sin(rp[...] + shift[LINES * c + 2 * p + i] * planes[3])
                matched = jnp.concatenate(
                    [
                        (re * cosine + im * sine).astype(BF16),
                        (im * cosine - re * sine).astype(BF16),
                    ],
                    axis=1,
                )
                w = dot(matched, outer[...])
                re, im = w[:, :R2], w[:, R2:]
                cosine, sine = planes[0], planes[1]
                parts.append(
                    jnp.concatenate(
                        [
                            (re * cosine - im * sine).astype(BF16),
                            (re * sine + im * cosine).astype(BF16),
                        ],
                        axis=0,
                    )
                )
            done = dot(last[...], jnp.concatenate(parts, axis=1)).astype(BF16)
            for i in range(2):
                for a in range(2):
                    rows[2 * p + i, a] = done[R1 * a : R1 * a + R1, R2 * i : R2 * i + R2]
            return 0

        lax.fori_loop(0, LINES // 2, two_lines, 0, unroll=4)

        def swapped(t, _):
            cut = [
                rows[:, :, pl.ds(pl.multiple_of(32 * t + 16 * i, 16), 16)].reshape(256, R2)
                for i in range(2)
            ]
            out = dot(swap[...], jnp.concatenate(cut, axis=1)).astype(BF16)
            for i in range(2):
                send[c, pl.ds(32 * t + 16 * i, 16)] = out[:, R2 * i : R2 * i + R2].reshape(16, 16, R2)
            return 0

        lax.fori_loop(0, 8, swapped, 0, unroll=2)
        if not talk:
            return 0

        @pl.when(c == 0)
        def _():
            pl.semaphore_wait(barrier, 255)

        pltpu.make_async_copy(send.at[c, me], out_hbm.at[c, me], own_sem).start()

        def sends(j, _):
            dy = lax.rem(j, 4)
            other = focus + dy
            other = jnp.where(other >= 4, other - 4, other)
            base = form + lax.div(j, 4)
            for dz in (4, 3, 5, 2, 6, 1, 7, 0):
                group = base + 8 * dz
                group = jnp.where(group >= 64, group - 64, group)

                def go():
                    pltpu.make_async_remote_copy(
                        src_ref=send.at[c, group * 4 + other],
                        dst_ref=out_hbm.at[c, me],
                        send_sem=send_sem,
                        recv_sem=recv_sem,
                        device_id=(group, other),
                        device_id_type=MESH,
                    ).start()

                if dz == 0:
                    pl.when(j > 0)(go)
                else:
                    go()
            return 0

        lax.fori_loop(0, 32, sends, 0)
        return 0

    lax.fori_loop(0, CHUNKS, chunk, 0)
    if not talk:
        copy = pltpu.make_async_copy(send, out_hbm, own_sem)
        copy.start()
        copy.wait()
        return
    pltpu.make_async_copy(send.at[:, 0], out_hbm.at[:, 0], own_sem).wait()
    pltpu.make_async_copy(send.at[:, pl.ds(0, 255)], out_hbm.at[:, pl.ds(0, 255)], send_sem).wait()
    pltpu.make_async_copy(send.at[:, pl.ds(0, 255)], out_hbm.at[:, pl.ds(0, 255)], recv_sem).wait()


def corner_turned(echoes, rate, shift, range_phase, talk=True):
    phase = range_phase.reshape(R2, R1)
    tables = range_tables()
    vmem = pl.BlockSpec(memory_space=pltpu.VMEM)
    smem = pl.BlockSpec(memory_space=pltpu.SMEM)
    hbm = pl.BlockSpec(memory_space=pl.ANY)
    return pl.pallas_call(
        functools.partial(range_kernel, talk=talk),
        out_shape=jax.ShapeDtypeStruct((CHUNKS, 256, 2 * LINES, R2), BF16),
        in_specs=[hbm, smem, smem, vmem] + [hbm] * 7,
        out_specs=hbm,
        scratch_shapes=[
            *[pltpu.VMEM(t.shape, t.dtype) for t in tables],
            pltpu.VMEM((2, 2, 16, R1 * R2), BF16),
            pltpu.VMEM((2, 16, R1, R2), BF16),
            pltpu.VMEM((R1, R2), F32),
            pltpu.VMEM((LINES, 2, R1, R2), BF16),
            pltpu.VMEM((CHUNKS, 256, 2 * LINES, R2), BF16),
            pltpu.SemaphoreType.DMA((2,)),
            pltpu.SemaphoreType.DMA((7,)),
            pltpu.SemaphoreType.DMA,
            pltpu.SemaphoreType.DMA,
            pltpu.SemaphoreType.DMA,
        ],
        compiler_params=pltpu.CompilerParams(
            has_side_effects=True, vmem_limit_bytes=62 * 2**20, **({"collective_id": 0} if talk else {})
        ),
        cost_estimate=pl.CostEstimate(flops=7 * 10**9, bytes_accessed=10**7, transcendentals=0),
        name="range_lines",
    )(echoes, rate, shift, phase, *[jnp.asarray(t) for t in tables])


def azimuth_kernel(
    r_hbm, t1, t2, t3, t4, t5, t6, rate, listed, held, img_hbm, terms,
    r, y, z, back, v, first, second, third, fourth, fifth, sixth, img, sums, sel, centers, sems, tab_sems, out_sem, *, split=True,
):
    loads = [
        pltpu.make_async_copy(r_hbm.at[pl.ds(2 * h, 2)], r.at[pl.ds(2 * h, 2)], sems.at[h])
        for h in range(2)
    ]
    tables = [
        pltpu.make_async_copy(a, b, tab_sems.at[i])
        for i, (a, b) in enumerate(
            [(t1, first), (t2, second), (t3, third), (t4, fourth), (t5, fifth), (t6, sixth)]
        )
    ]
    tables[0].start()
    loads[0].start()
    loads[1].start()
    for i in range(1, 6):
        tables[i].start()

    own = lax.axis_index("focus") * R2 if split else 0
    centers[...] = jnp.zeros((2, R2), jnp.int32) - 1
    centers[0:1, :LISTED] = held[...]
    centers[1:2, :LISTED] = listed[...] - own
    column = lax.broadcasted_iota(jnp.int32, (R2, R2), 0)
    sel[...] = jnp.where(column == centers[1:2], 1.0, 0.0).astype(BF16)

    def pair(one, other):
        return jnp.concatenate([one.reshape(256, R2), other.reshape(256, R2)], axis=1)

    def halves(out):
        out = out.astype(BF16)
        return [out[:, R2 * i : R2 * i + R2].reshape(16, 16, R2) for i in range(2)]

    def forward(wait):
        for h in range(2):
            if wait:
                if h == 0:
                    tables[0].wait()
                loads[h].wait()

            def one(s, _):
                out = halves(dot(first[s], pair(r[2 * h, :, s], r[2 * h + 1, :, s])))
                for i in range(2):
                    y[2 * h + i, :, s] = out[i]
                return 0

            lax.fori_loop(0, 16, one, 0, unroll=4)
        if wait:
            tables[1].wait()
        for c in range(CHUNKS):

            def two(k, _):
                out = halves(dot(second[c], pair(y[c, 2 * k], y[c, 2 * k + 1])))
                for i in range(2):
                    z[:, 2 * k + i, c] = out[i]
                return 0

            lax.fori_loop(0, 8, two, 0, unroll=4)

    def spectrum(k, h):
        return dot(third[k], pair(z[pl.ds(8 * h, 4), k], z[pl.ds(8 * h + 4, 4), k]))

    forward(True)
    for i in range(2, 6):
        tables[i].wait()
    m = lax.broadcasted_iota(jnp.int32, (32, R2), 0)
    m = jnp.where(m >= 16, m - 32, m).astype(F32) * (1.0 / 32)
    cycles = rate[...] * (1.0 / TWO_PI)

    def filtered(j, _):
        k, h = lax.div(j, 2), lax.rem(j, 2)
        out = spectrum(k, h)
        columns = []
        for i in range(2):
            rows = []
            for x in range(4):
                re = out[64 * x : 64 * x + 32, R2 * i : R2 * i + R2]
                im = out[64 * x + 32 : 64 * x + 64, R2 * i : R2 * i + R2]
                f = m + (k + 16 * (8 * h + 4 * i + x)).astype(F32) * (1.0 / AZ)
                cosine, sine = cos_sin(f * f * cycles)
                rows.append((re * cosine + im * sine).astype(BF16))
                rows.append((im * cosine - re * sine).astype(BF16))
            columns.append(jnp.concatenate(rows, axis=0))
        out = dot(fourth[k], jnp.concatenate(columns, axis=1)).astype(BF16)
        for i in range(2):
            back[pl.ds(8 * h + 4 * i, 4), k] = out[:, R2 * i : R2 * i + R2].reshape(4, 4, 16, R2)
        return 0

    lax.fori_loop(0, 32, filtered, 0, unroll=2)
    for c in range(CHUNKS):

        def three(k, _):
            out = halves(dot(fifth[c], pair(back[:, 2 * k, c], back[:, 2 * k + 1, c])))
            for i in range(2):
                y[c, :, 2 * k + i] = out[i]
            return 0

        lax.fori_loop(0, 8, three, 0, unroll=4)
    for h in range(2):

        def four(s, _):
            out = dot(sixth[s], pair(y[2 * h, s], y[2 * h + 1, s]))
            out = out.reshape(16, 2, LINES, 2 * R2)
            out = jnp.concatenate([out[..., :R2], out[..., R2:]], axis=2).astype(BF16)
            for a in range(2):
                img[a, :, s, 16 * h : 16 * h + 16] = out[:, a]
            return 0

        lax.fori_loop(0, 16, four, 0, unroll=4)
    image_out = pltpu.make_async_copy(img, img_hbm, out_sem)
    image_out.start()

    line = lax.broadcasted_iota(jnp.int32, (256, R2), 0)

    def windowed(t, _):
        hi, lo = lax.div(t, 2), lax.rem(t, 2) * 8
        away = jnp.bitwise_and(line + 256 * t - centers[0:1], AZ - 1)
        away = jnp.minimum(away, AZ - away).astype(F32)
        window = jnp.maximum(1.0 - away * (16.0 / AZ), 0.0)
        parts = [
            (dot(img[a, hi, pl.ds(lo, 8)].reshape(256, R2), sel[...]) * window).reshape(8, 4, 1, LINES, R2)
            for a in range(2)
        ]
        both = jnp.concatenate(parts, axis=2).astype(BF16)
        for c in range(CHUNKS):
            r[c, hi, pl.ds(lo, 8)] = both[:, c].reshape(8, 16, R2)
        return 0

    lax.fori_loop(0, 32, windowed, 0, unroll=2)
    forward(False)

    def line_spectrum(j, _):
        k, h = lax.div(j, 2), lax.rem(j, 2)
        out = spectrum(k, h)
        for i in range(2):
            v[pl.ds(8 * h + 4 * i, 4), k] = out[:, R2 * i : R2 * i + R2].reshape(4, 2, 32, R2)
        return 0

    lax.fori_loop(0, 32, line_spectrum, 0, unroll=4)
    end_re, end_im = pltpu.roll(v[0, 0, 0], 31, 0), pltpu.roll(v[0, 0, 1], 31, 0)

    def group(g, _):
        cross = jnp.zeros((32, R2), F32)
        energy = jnp.zeros((32, R2), F32)
        re, im = v[2 * g, 0, 0], v[2 * g, 0, 1]
        for i in range(1, 33):
            k2 = 2 * g + i // 16
            if i == 32:
                k2 = lax.rem(k2, 16)
            next_re, next_im = v[k2, i % 16, 0], v[k2, i % 16, 1]
            if i == 32:
                next_re = jnp.where(g == 7, end_re, next_re)
                next_im = jnp.where(g == 7, end_im, next_im)
            cross += re * next_im - im * next_re
            energy += re * re + im * im
            re, im = next_re, next_im
        sums[pl.ds(g, 32, stride=8)] = cross
        sums[pl.ds(256 + g, 32, stride=8)] = energy
        return 0

    lax.fori_loop(0, 8, group, 0)
    terms[...] = sums[...].T[:LISTED]
    image_out.wait()


def focused(arrived, rate, listed, held, split=True):
    vmem = pl.BlockSpec(memory_space=pltpu.VMEM)
    hbm = pl.BlockSpec(memory_space=pl.ANY)
    tables = azimuth_tables()
    image, terms = pl.pallas_call(
        functools.partial(azimuth_kernel, split=split),
        out_shape=(
            jax.ShapeDtypeStruct((2, 16, 16, 32, R2), BF16),
            jax.ShapeDtypeStruct((LISTED, 512), F32),
        ),
        in_specs=[hbm] * 7 + [vmem] * 3,
        out_specs=(hbm, vmem),
        scratch_shapes=[
            pltpu.VMEM((4, 16, 16, 16, R2), BF16),
            pltpu.VMEM((4, 16, 16, 16, R2), BF16),
            pltpu.VMEM((16, 16, 4, 16, R2), BF16),
            pltpu.VMEM((16, 16, 4, 16, R2), BF16),
            pltpu.VMEM((16, 16, 2, 32, R2), F32),
            *[pltpu.VMEM(t.shape, BF16) for t in tables],
            pltpu.VMEM((2, 16, 16, 32, R2), BF16),
            pltpu.VMEM((512, R2), F32),
            pltpu.VMEM((R2, R2), BF16),
            pltpu.VMEM((2, R2), jnp.int32),
            pltpu.SemaphoreType.DMA((2,)),
            pltpu.SemaphoreType.DMA((6,)),
            pltpu.SemaphoreType.DMA,
        ],
        compiler_params=pltpu.CompilerParams(vmem_limit_bytes=62 * 2**20),
        cost_estimate=pl.CostEstimate(flops=15 * 10**9, bytes_accessed=2 * 10**7, transcendentals=0),
        name="azimuth_columns",
    )(arrived.reshape(4, 16, 16, 16, R2), *[jnp.asarray(t) for t in tables], rate[None], listed, held)
    return image.reshape(2, AZ, R2), terms


def map_kernel(terms, blocks, out, got, rows, parts, send_sem, recv_sem, row_send, row_recv):
    form = lax.axis_index("form")
    focus = lax.axis_index("focus")
    barrier = pltpu.get_barrier_semaphore()
    for d in range(1, 4):
        other = focus + d
        other = jnp.where(other >= 4, other - 4, other)
        pl.semaphore_signal(barrier, inc=1, device_id=(form, other), device_id_type=MESH)

    def greet(j, _):
        for dz in range(8):
            other = form + j + 8 * dz
            other = jnp.where(other >= 64, other - 64, other)

            def hello():
                pl.semaphore_signal(barrier, inc=1, device_id=(other, focus), device_id_type=MESH)

            if dz == 0:
                pl.when(j > 0)(hello)
            else:
                hello()
        return 0

    lax.fori_loop(0, 8, greet, 0)
    own = 4 * lax.broadcasted_iota(jnp.int32, (64, LISTED), 0) + focus
    chosen = jnp.where(own == blocks[...], 1.0, 0.0)
    pl.semaphore_wait(barrier, 66)
    copies = []
    for d in range(1, 4):
        other = focus + d
        other = jnp.where(other >= 4, other - 4, other)
        copies.append(
            pltpu.make_async_remote_copy(
                src_ref=terms,
                dst_ref=got.at[d - 1],
                send_sem=send_sem.at[d - 1],
                recv_sem=recv_sem.at[d - 1],
                device_id=(form, other),
                device_id_type=MESH,
            )
        )
        copies[-1].start()
    for copy in copies:
        copy.wait_recv()
    group = terms[...] + got[0] + (got[1] + got[2])
    mine = jnp.dot(
        chosen, group, preferred_element_type=F32, precision=lax.Precision.HIGHEST
    )
    for i in range(4):
        rows[:, i] = mine[:, R2 * i : R2 * i + R2]
    parts[form] = rows[form]

    def sends(j, _):
        for dz in (4, 3, 5, 2, 6, 1, 7, 0):
            other = form + j + 8 * dz
            other = jnp.where(other >= 64, other - 64, other)

            def go():
                pltpu.make_async_remote_copy(
                    src_ref=rows.at[other],
                    dst_ref=parts.at[form],
                    send_sem=row_send,
                    recv_sem=row_recv,
                    device_id=(other, focus),
                    device_id_type=MESH,
                ).start()

            if dz == 0:
                pl.when(j > 0)(go)
            else:
                go()
        return 0

    lax.fori_loop(0, 8, sends, 0)
    for copy in copies:
        copy.wait_send()
    pltpu.make_async_copy(rows.at[pl.ds(0, 63)], parts.at[pl.ds(0, 63)], row_send).wait()
    pltpu.make_async_copy(rows.at[pl.ds(0, 63)], parts.at[pl.ds(0, 63)], row_recv).wait()
    total = jnp.sum(parts[...], axis=0)
    out[...] = total[:2] / (total[2:] + EPSILON)


def own_map(terms, blocks):
    vmem = pl.BlockSpec(memory_space=pltpu.VMEM)
    return pl.pallas_call(
        map_kernel,
        out_shape=jax.ShapeDtypeStruct((2, R2), F32),
        in_specs=[vmem, vmem],
        out_specs=vmem,
        scratch_shapes=[
            pltpu.VMEM((3, LISTED, 512), F32),
            pltpu.VMEM((64, 4, R2), F32),
            pltpu.VMEM((64, 4, R2), F32),
            pltpu.SemaphoreType.DMA((3,)),
            pltpu.SemaphoreType.DMA((3,)),
            pltpu.SemaphoreType.DMA,
            pltpu.SemaphoreType.DMA,
        ],
        compiler_params=pltpu.CompilerParams(
            has_side_effects=True, vmem_limit_bytes=62 * 2**20, collective_id=1
        ),
        name="phase_rows",
    )(terms, blocks)


def on_device(
    echoes,
    scale_rate,
    migration,
    range_phase,
    azimuth_rate,
    bright_columns,
    line_block,
    line_center,
):
    arrived = corner_turned(echoes, scale_rate, migration, range_phase)
    focused_image, terms = focused(arrived, azimuth_rate, bright_columns, line_center)
    phase_map = own_map(terms, line_block.reshape(1, LISTED)).reshape(1, 256)
    return (focused_image, phase_map)


def solution(mesh):
    in_specs = (
        P(None, ("form", "focus"), None),
        P(("form", "focus")),
        P(("form", "focus")),
        P(),
        P(("form", "focus")),
        P("form", None),
        P("form", None, None),
        P("form", None),
    )
    out_specs = (P(None, None, ("form", "focus")), P(("form", "focus"), None))
    return jax.shard_map(
        on_device, mesh=mesh, in_specs=in_specs, out_specs=out_specs, check_vma=False
    )
```

```python
import functools
import math

import jax
import jax.numpy as jnp
import ml_dtypes
import numpy as np
from jax import lax
from jax.experimental import pallas as pl
from jax.experimental.pallas import tpu as pltpu
from jax.sharding import PartitionSpec as P

R1 = 256
R2 = 128
NBLK = 256
AZ = 8192
CHUNKS = 4
LISTED = 32
LINES = 8
MESH = pl.DeviceIdType.MESH
F32 = jnp.float32
BF16 = jnp.bfloat16

TWO_PI = 2.0 * math.pi
EPSILON = 1e-06


def real_blocks(values):
    upper = np.stack([values.real, -values.imag], axis=-2)
    lower = np.stack([values.imag, values.real], axis=-2)
    return np.stack([upper, lower], axis=-4)


def unit(turns):
    return np.exp(2j * np.pi * turns)


def range_tables():
    k = np.arange(R1)
    n = np.arange(R2)
    wide = np.outer(k, k) % R1 / R1
    narrow = np.outer(n, n) % R2 / R2
    first = real_blocks(unit(-wide) / 16).reshape(2 * R1, 2 * R1)
    last = real_blocks(unit(wide) / 16).reshape(2 * R1, 2 * R1)
    inner = real_blocks(unit(-narrow) / math.sqrt(R2)).reshape(2 * R2, 2 * R2).T
    outer = real_blocks(unit(narrow) / math.sqrt(R2)).reshape(2 * R2, 2 * R2).T
    twist = unit(np.outer(k, n) / (R1 * R2))
    length = R1 * R2
    offsets = (k[:, None] * R2 + n[None, :] - length // 2) / length
    bins = k[:, None] + R1 * n[None, :]
    signed = np.where(bins >= length // 2, bins - length, bins) / length
    planes = np.stack([twist.real, twist.imag, offsets * offsets / TWO_PI, signed])
    swap = np.eye(256).reshape(LINES, 2, 16, 256).transpose(2, 1, 0, 3).reshape(256, 256)
    cross = np.eye(256).reshape(16, 16, 256).transpose(1, 0, 2).reshape(256, 256)
    half = [t.astype(ml_dtypes.bfloat16) for t in (first, inner, outer, last, swap, cross)]
    return half + [planes.astype(np.float32)]


def azimuth_tables():
    i = np.arange(16)
    near = np.outer(i, i) / 16
    shift = np.outer(i, i) / 256
    l8, m = np.arange(LINES), np.arange(32)
    eye = np.eye(LINES)

    def widened(turns):
        blocks = real_blocks(np.moveaxis(unit(turns) / 4, -1, 0))
        full = np.einsum("l...atcf,lm->...talfcm", blocks, eye)
        return full.reshape(*full.shape[:-6], 256, 256)

    same = np.zeros(LINES)
    lines = LINES * np.arange(CHUNKS)[:, None] + l8
    first = widened(-(near[None] + shift[:, :, None])[..., None] - same)
    second = widened(-near[None, :, :, None] - (i[:, None] * lines[:, None, :] / 512)[:, :, None, :])
    part = (lines[None] * i[:, None, None] / AZ)[:, None] + (lines * m[:, None, None] / 32)[None]
    wide = real_blocks((unit(-part) / math.sqrt(32)).reshape(16, 32, 32)).reshape(16, 2, 32, 2, CHUNKS, LINES)
    third = np.einsum("kamchl,xy->kxamyhcl", wide, np.eye(4)).reshape(16, 256, 256)
    wide = real_blocks((unit(part) / math.sqrt(32)).transpose(0, 2, 3, 1).reshape(16, 32, 32))
    wide = wide.reshape(16, 2, CHUNKS, LINES, 2, 32)
    fourth = np.einsum("kahlcm,xy->kxhalycm", wide, np.eye(4)).reshape(16, 256, 256)
    fifth = widened(near[None, :, :, None] + (i[:, None] * lines[:, None, :] / 512)[:, None, :, :])
    sixth = widened((near[None] + shift[:, None, :])[..., None] + same)
    return [t.astype(ml_dtypes.bfloat16) for t in (first, second, third, fourth, fifth, sixth)]


def cos_sin(turns):
    rest = turns - jnp.round(turns)
    z = rest * rest
    sine = rest * (6.28316395 + z * (-10.3342826 + z * (5.08377413 - 1.1092177 * z)))
    cosine = 0.99999995 + z * (-4.93479283 + z * (4.05841135 + z * (-1.33187657 + 0.21968961 * z)))
    return 1.0 - 0.5 * (sine * sine), sine * cosine


def dot(a, b):
    return jnp.dot(a, b, preferred_element_type=F32)


def pair(one, other):
    return jnp.concatenate([one.reshape(256, R2), other.reshape(256, R2)], axis=1)


def halves(out):
    out = out.astype(BF16)
    return [out[:, R2 * i : R2 * i + R2].reshape(16, 16, R2) for i in range(2)]


def first_stages(h, r, y, z, first, second):
    def one(s, _):
        out = halves(dot(first[s], pair(r[2 * h, :, s], r[2 * h + 1, :, s])))
        for i in range(2):
            y[2 * h + i, :, s] = out[i]
        return 0

    lax.fori_loop(0, 16, one, 0, unroll=4)
    for c in (2 * h, 2 * h + 1):

        def two(k, _):
            out = halves(dot(second[c], pair(y[c, 2 * k], y[c, 2 * k + 1])))
            for i in range(2):
                z[:, 2 * k + i, c] = out[i]
            return 0

        lax.fori_loop(0, 8, two, 0, unroll=4)


def range_kernel(
    x_hbm, rate, shift, phase, *args, talk=True,
):
    sources, out_hbm, tables = args[:9], args[9], args[10:19]
    raw, xbuf, rp, rows, send, got, y, z, in_sem, tab_sem, send_sem, recv_sem, own_sem, out_sem = args[19:]
    first, inner, outer, last, swap, cross, planes, az_first, az_second = tables
    loads = [
        pltpu.make_async_copy(x_hbm.at[:, pl.ds(16 * h, 16)], raw.at[h], in_sem.at[h]) for h in range(2)
    ]
    copies = [pltpu.make_async_copy(a, b, tab_sem.at[i]) for i, (a, b) in enumerate(zip(sources, tables))]
    loads[0].start()
    for i in (5, 6, 0, 1, 2, 3, 4):
        copies[i].start()
    loads[1].start()
    copies[7].start()
    copies[8].start()
    for i in range(2):
        rp[R2 * i : R2 * i + R2] = phase[pl.ds(i, R2, stride=2), :].T * (1.0 / TWO_PI)
    copies[5].wait()
    if talk:
        form = lax.axis_index("form")
        focus = lax.axis_index("focus")
        me = form * 4 + focus
        me_hi, me_lo = lax.div(me, 16), lax.rem(me, 16)
        barrier = pltpu.get_barrier_semaphore()

        def greet(j, _):
            for d in range(8):
                group = form + j + 8 * d
                group = jnp.where(group >= 64, group - 64, group)
                for dy in range(4):
                    other = focus + dy
                    other = jnp.where(other >= 4, other - 4, other)

                    def hello():
                        pl.semaphore_signal(
                            barrier, inc=1, device_id=(group, other), device_id_type=MESH
                        )

                    if d == 0 and dy == 0:
                        pl.when(j > 0)(hello)
                    else:
                        hello()
            return 0

        lax.fori_loop(0, 8, greet, 0)

    def chunk(c, _):
        h = lax.div(c, 2)

        @pl.when(lax.rem(c, 2) == 0)
        def _():
            pltpu.make_async_copy(x_hbm.at[:, pl.ds(16 * h, 16)], raw.at[h], in_sem.at[h]).wait()

            def unfold(t, _):
                cut = [
                    jnp.concatenate(
                        [
                            raw[h, a, :, pl.ds(pl.multiple_of(2048 * t + R2 * i, R2), R2)]
                            for i in range(16)
                        ],
                        axis=0,
                    )
                    for a in range(2)
                ]
                out = dot(cross[...], jnp.concatenate(cut, axis=1)).astype(BF16)
                for a in range(2):
                    xbuf[a, :, pl.ds(pl.multiple_of(16 * t, 16), 16)] = out[
                        :, R2 * a : R2 * a + R2
                    ].reshape(16, 16, R2)
                return 0

            lax.fori_loop(0, 16, unfold, 0, unroll=4)

        @pl.when(c == 0)
        def _():
            for i in (6, 0, 1, 2, 3, 4):
                copies[i].wait()

        half = LINES * lax.rem(c, 2)

        def two_lines(p, _):
            parts = []
            for i in range(2):
                l = 2 * p + i
                cosine, sine = cos_sin(rate[LINES * c + l] * planes[2])
                re = xbuf[0, half + l].astype(F32)
                im = xbuf[1, half + l].astype(F32)
                parts.append(
                    jnp.concatenate(
                        [
                            (re * cosine - im * sine).astype(BF16),
                            (re * sine + im * cosine).astype(BF16),
                        ],
                        axis=0,
                    )
                )
            u = dot(first[...], jnp.concatenate(parts, axis=1))
            parts = []
            for i in range(2):
                lanes = slice(R2 * i, R2 * i + R2)
                re, im = u[:R1, lanes], u[R1:, lanes]
                cosine, sine = planes[0], planes[1]
                twisted = jnp.concatenate(
                    [
                        (re * cosine + im * sine).astype(BF16),
                        (im * cosine - re * sine).astype(BF16),
                    ],
                    axis=1,
                )
                spectrum = dot(twisted, inner[...])
                re, im = spectrum[:, :R2], spectrum[:, R2:]
                cosine, sine = cos_sin(rp[...] + shift[LINES * c + 2 * p + i] * planes[3])
                matched = jnp.concatenate(
                    [
                        (re * cosine + im * sine).astype(BF16),
                        (im * cosine - re * sine).astype(BF16),
                    ],
                    axis=1,
                )
                w = dot(matched, outer[...])
                re, im = w[:, :R2], w[:, R2:]
                cosine, sine = planes[0], planes[1]
                parts.append(
                    jnp.concatenate(
                        [
                            (re * cosine - im * sine).astype(BF16),
                            (re * sine + im * cosine).astype(BF16),
                        ],
                        axis=0,
                    )
                )
            done = dot(last[...], jnp.concatenate(parts, axis=1)).astype(BF16)
            for i in range(2):
                for a in range(2):
                    rows[2 * p + i, a] = done[R1 * a : R1 * a + R1, R2 * i : R2 * i + R2]
            return 0

        lax.fori_loop(0, LINES // 2, two_lines, 0, unroll=4)

        def swapped(t, _):
            cut = [
                rows[:, :, pl.ds(pl.multiple_of(32 * t + 16 * i, 16), 16)].reshape(256, R2)
                for i in range(2)
            ]
            out = dot(swap[...], jnp.concatenate(cut, axis=1)).astype(BF16)
            for i in range(2):
                send[c, pl.ds(32 * t + 16 * i, 16)] = out[:, R2 * i : R2 * i + R2].reshape(16, 16, R2)
            return 0

        lax.fori_loop(0, 8, swapped, 0, unroll=2)
        if not talk:
            return 0

        @pl.when(c == 0)
        def _():
            pl.semaphore_wait(barrier, 255)

        pltpu.make_async_copy(send.at[c, me], got.at[c, me_hi, me_lo], own_sem.at[c]).start()

        def sends(j, _):
            dy = lax.rem(j, 4)
            other = focus + dy
            other = jnp.where(other >= 4, other - 4, other)
            base = form + lax.div(j, 4)
            for dz in (4, 3, 5, 2, 6, 1, 7, 0):
                group = base + 8 * dz
                group = jnp.where(group >= 64, group - 64, group)

                def go():
                    pltpu.make_async_remote_copy(
                        src_ref=send.at[c, group * 4 + other],
                        dst_ref=got.at[c, me_hi, me_lo],
                        send_sem=send_sem,
                        recv_sem=recv_sem.at[c],
                        device_id=(group, other),
                        device_id_type=MESH,
                    ).start()

                if dz == 0:
                    pl.when(j > 0)(go)
                else:
                    go()
            return 0

        lax.fori_loop(0, 32, sends, 0)
        return 0

    lax.fori_loop(0, CHUNKS, chunk, 0)
    for h in range(2):
        if h == 0:
            copies[7].wait()
            copies[8].wait()
        if talk:
            for c in (2 * h, 2 * h + 1):
                pltpu.make_async_copy(send.at[c, 0], got.at[c, 0, 0], own_sem.at[c]).wait()
                pltpu.make_async_copy(
                    send.at[c, pl.ds(0, 255)], send.at[c, pl.ds(0, 255)], recv_sem.at[c]
                ).wait()
        first_stages(h, got, y, z, az_first, az_second)
        pltpu.make_async_copy(
            z.at[:, :, pl.ds(2 * h, 2)], out_hbm.at[:, :, pl.ds(2 * h, 2)], out_sem.at[h]
        ).start()
    if talk:
        pltpu.make_async_copy(send.at[:, pl.ds(0, 255)], send.at[:, pl.ds(0, 255)], send_sem).wait()
    for h in range(2):
        pltpu.make_async_copy(
            z.at[:, :, pl.ds(2 * h, 2)], out_hbm.at[:, :, pl.ds(2 * h, 2)], out_sem.at[h]
        ).wait()


def corner_turned(echoes, rate, shift, range_phase, talk=True):
    phase = range_phase.reshape(R1, R2)
    tables = range_tables() + azimuth_tables()[:2]
    vmem = pl.BlockSpec(memory_space=pltpu.VMEM)
    smem = pl.BlockSpec(memory_space=pltpu.SMEM)
    hbm = pl.BlockSpec(memory_space=pl.ANY)
    return pl.pallas_call(
        functools.partial(range_kernel, talk=talk),
        out_shape=jax.ShapeDtypeStruct((16, 16, CHUNKS, 16, R2), BF16),
        in_specs=[hbm, smem, smem, vmem] + [hbm] * 9,
        out_specs=hbm,
        scratch_shapes=[
            *[pltpu.VMEM(t.shape, t.dtype) for t in tables],
            pltpu.VMEM((2, 2, 16, R1 * R2), BF16),
            pltpu.VMEM((2, 16, R1, R2), BF16),
            pltpu.VMEM((R1, R2), F32),
            pltpu.VMEM((LINES, 2, R1, R2), BF16),
            pltpu.VMEM((CHUNKS, 256, 2 * LINES, R2), BF16),
            pltpu.VMEM((CHUNKS, 16, 16, 16, R2), BF16),
            pltpu.VMEM((CHUNKS, 16, 16, 16, R2), BF16),
            pltpu.VMEM((16, 16, CHUNKS, 16, R2), BF16),
            pltpu.SemaphoreType.DMA((2,)),
            pltpu.SemaphoreType.DMA((9,)),
            pltpu.SemaphoreType.DMA,
            pltpu.SemaphoreType.DMA((CHUNKS,)),
            pltpu.SemaphoreType.DMA((CHUNKS,)),
            pltpu.SemaphoreType.DMA((2,)),
        ],
        compiler_params=pltpu.CompilerParams(
            has_side_effects=True, vmem_limit_bytes=62 * 2**20, **({"collective_id": 0} if talk else {})
        ),
        cost_estimate=pl.CostEstimate(flops=7 * 10**9, bytes_accessed=10**7, transcendentals=0),
        name="range_lines",
    )(echoes, rate, shift, phase, *[jnp.asarray(t) for t in tables])


def azimuth_kernel(
    z_hbm, t1, t2, t3, t4, t5, t6, rate, listed, held, img_hbm, terms,
    r, y, z, back, v, first, second, third, fourth, fifth, sixth, img, sums, sel, centers, sems, tab_sems, out_sem, *, split=True,
):
    def batch(g):
        part = pl.ds(4 * g, 4)
        refs = [(z_hbm.at[:, part], z.at[:, part]), (t3.at[part], third.at[part]), (t4.at[part], fourth.at[part])]
        return [pltpu.make_async_copy(a, b, sems.at[g, i]) for i, (a, b) in enumerate(refs)]

    for g in range(4):
        for copy in batch(g):
            copy.start()
    tables = [
        pltpu.make_async_copy(a, b, tab_sems.at[i])
        for i, (a, b) in enumerate([(t5, fifth), (t6, sixth), (t1, first), (t2, second)])
    ]
    for copy in tables:
        copy.start()
    own = lax.axis_index("focus") * R2 if split else 0
    centers[...] = jnp.zeros((2, R2), jnp.int32) - 1
    centers[0:1, :LISTED] = held[...]
    centers[1:2, :LISTED] = listed[...] - own
    column = lax.broadcasted_iota(jnp.int32, (R2, R2), 0)
    sel[...] = jnp.where(column == centers[1:2], 1.0, 0.0).astype(BF16)

    def spectrum(k, h):
        return dot(third[k], pair(z[pl.ds(8 * h, 4), k], z[pl.ds(8 * h + 4, 4), k]))

    m = lax.broadcasted_iota(jnp.int32, (32, R2), 0)
    m = jnp.where(m >= 16, m - 32, m).astype(F32) * (1.0 / 32)
    cycles = rate[...] * (1.0 / TWO_PI)

    def filtered(j, _):
        k, h = lax.div(j, 2), lax.rem(j, 2)
        out = spectrum(k, h)
        columns = []
        for i in range(2):
            rows = []
            for x in range(4):
                re = out[64 * x : 64 * x + 32, R2 * i : R2 * i + R2]
                im = out[64 * x + 32 : 64 * x + 64, R2 * i : R2 * i + R2]
                f = m + (k + 16 * (8 * h + 4 * i + x)).astype(F32) * (1.0 / AZ)
                cosine, sine = cos_sin(f * f * cycles)
                rows.append((re * cosine + im * sine).astype(BF16))
                rows.append((im * cosine - re * sine).astype(BF16))
            columns.append(jnp.concatenate(rows, axis=0))
        out = dot(fourth[k], jnp.concatenate(columns, axis=1)).astype(BF16)
        for i in range(2):
            back[pl.ds(8 * h + 4 * i, 4), k] = out[:, R2 * i : R2 * i + R2].reshape(4, 4, 16, R2)
        return 0

    for g in range(4):
        for copy in batch(g):
            copy.wait()
        lax.fori_loop(8 * g, 8 * g + 8, filtered, 0, unroll=2)
    tables[0].wait()
    tables[1].wait()
    for c in range(CHUNKS):

        def three(k, _):
            out = halves(dot(fifth[c], pair(back[:, 2 * k, c], back[:, 2 * k + 1, c])))
            for i in range(2):
                y[c, :, 2 * k + i] = out[i]
            return 0

        lax.fori_loop(0, 8, three, 0, unroll=4)
    for h in range(2):

        def four(s, _):
            out = dot(sixth[s], pair(y[2 * h, s], y[2 * h + 1, s]))
            out = out.reshape(16, 2, LINES, 2 * R2)
            out = jnp.concatenate([out[..., :R2], out[..., R2:]], axis=2).astype(BF16)
            for a in range(2):
                img[a, :, s, 16 * h : 16 * h + 16] = out[:, a]
            return 0

        lax.fori_loop(0, 16, four, 0, unroll=4)
    image_out = pltpu.make_async_copy(img, img_hbm, out_sem)
    image_out.start()

    line = lax.broadcasted_iota(jnp.int32, (256, R2), 0)

    def windowed(t, _):
        hi, lo = lax.div(t, 2), lax.rem(t, 2) * 8
        away = jnp.bitwise_and(line + 256 * t - centers[0:1], AZ - 1)
        away = jnp.minimum(away, AZ - away).astype(F32)
        window = jnp.maximum(1.0 - away * (16.0 / AZ), 0.0)
        parts = [
            (dot(img[a, hi, pl.ds(lo, 8)].reshape(256, R2), sel[...]) * window).reshape(8, 4, 1, LINES, R2)
            for a in range(2)
        ]
        both = jnp.concatenate(parts, axis=2).astype(BF16)
        for c in range(CHUNKS):
            r[c, hi, pl.ds(lo, 8)] = both[:, c].reshape(8, 16, R2)
        return 0

    lax.fori_loop(0, 32, windowed, 0, unroll=2)
    tables[2].wait()
    tables[3].wait()
    for h in range(2):
        first_stages(h, r, y, z, first, second)

    def line_spectrum(j, _):
        k, h = lax.div(j, 2), lax.rem(j, 2)
        out = spectrum(k, h)
        for i in range(2):
            v[pl.ds(8 * h + 4 * i, 4), k] = out[:, R2 * i : R2 * i + R2].reshape(4, 2, 32, R2)
        return 0

    lax.fori_loop(0, 32, line_spectrum, 0, unroll=4)
    end_re, end_im = pltpu.roll(v[0, 0, 0], 31, 0), pltpu.roll(v[0, 0, 1], 31, 0)

    def group(g, _):
        cross = jnp.zeros((32, R2), F32)
        energy = jnp.zeros((32, R2), F32)
        re, im = v[2 * g, 0, 0], v[2 * g, 0, 1]
        for i in range(1, 33):
            k2 = 2 * g + i // 16
            if i == 32:
                k2 = lax.rem(k2, 16)
            next_re, next_im = v[k2, i % 16, 0], v[k2, i % 16, 1]
            if i == 32:
                next_re = jnp.where(g == 7, end_re, next_re)
                next_im = jnp.where(g == 7, end_im, next_im)
            cross += re * next_im - im * next_re
            energy += re * re + im * im
            re, im = next_re, next_im
        sums[pl.ds(g, 32, stride=8)] = cross
        sums[pl.ds(256 + g, 32, stride=8)] = energy
        return 0

    lax.fori_loop(0, 8, group, 0)
    terms[...] = sums[...].T[:LISTED].astype(BF16)
    image_out.wait()


def focused(arrived, rate, listed, held, split=True):
    vmem = pl.BlockSpec(memory_space=pltpu.VMEM)
    hbm = pl.BlockSpec(memory_space=pl.ANY)
    tables = azimuth_tables()
    image, terms = pl.pallas_call(
        functools.partial(azimuth_kernel, split=split),
        out_shape=(
            jax.ShapeDtypeStruct((2, 16, 16, 32, R2), BF16),
            jax.ShapeDtypeStruct((LISTED, 512), BF16),
        ),
        in_specs=[hbm] * 7 + [vmem] * 3,
        out_specs=(hbm, vmem),
        scratch_shapes=[
            pltpu.VMEM((4, 16, 16, 16, R2), BF16),
            pltpu.VMEM((4, 16, 16, 16, R2), BF16),
            pltpu.VMEM((16, 16, 4, 16, R2), BF16),
            pltpu.VMEM((16, 16, 4, 16, R2), BF16),
            pltpu.VMEM((16, 16, 2, 32, R2), F32),
            *[pltpu.VMEM(t.shape, BF16) for t in tables],
            pltpu.VMEM((2, 16, 16, 32, R2), BF16),
            pltpu.VMEM((512, R2), F32),
            pltpu.VMEM((R2, R2), BF16),
            pltpu.VMEM((2, R2), jnp.int32),
            pltpu.SemaphoreType.DMA((4, 3)),
            pltpu.SemaphoreType.DMA((4,)),
            pltpu.SemaphoreType.DMA,
        ],
        compiler_params=pltpu.CompilerParams(vmem_limit_bytes=62 * 2**20),
        cost_estimate=pl.CostEstimate(flops=15 * 10**9, bytes_accessed=2 * 10**7, transcendentals=0),
        name="azimuth_columns",
    )(arrived, *[jnp.asarray(t) for t in tables], rate[None], listed, held)
    return image.reshape(2, AZ, R2), terms


def map_kernel(terms, blocks, out, got, rows, parts, sums, ends, sems):
    form = lax.axis_index("form")
    focus = lax.axis_index("focus")
    row, ring = lax.rem(form, 8), lax.div(form, 8)

    def wrapped(value, size):
        return jnp.where(value >= size, value - size, value)

    mates = [(form, wrapped(focus + d, 4)) for d in range(1, 4)]
    across = [wrapped(row + d, 8) for d in range(1, 8)]
    along = [wrapped(ring + d, 8) for d in range(1, 8)]
    barrier = pltpu.get_barrier_semaphore()
    for peer in mates + [(ring * 8 + r, focus) for r in across] + [(z * 8 + row, focus) for z in along]:
        pl.semaphore_signal(barrier, inc=1, device_id=peer, device_id_type=MESH)
    place = lax.broadcasted_iota(jnp.int32, (64, LISTED), 0)
    own = (jnp.bitwise_and(place, 7) * 8 + jnp.right_shift(place, 3)) * 4 + focus
    chosen = jnp.where(own == blocks[...], 1.0, 0.0).astype(BF16)
    pl.semaphore_wait(barrier, 17)

    def send(src, dst, i, peer):
        copy = pltpu.make_async_remote_copy(
            src_ref=src,
            dst_ref=dst,
            send_sem=sems.at[2 * i],
            recv_sem=sems.at[2 * i + 1],
            device_id=peer,
            device_id_type=MESH,
        )
        copy.start()
        return copy

    started = [send(terms, got.at[d], d, mates[d]) for d in range(3)]
    for copy in started:
        copy.wait_recv()
    group = terms[...].astype(F32) + got[0].astype(F32) + (got[1].astype(F32) + got[2].astype(F32))
    mine = dot(chosen, group.astype(BF16))
    for i in range(4):
        rows[:, i] = mine[:, R2 * i : R2 * i + R2]
    second = [
        send(rows.at[pl.ds(8 * r, 8)], parts.at[d], 3 + d, (ring * 8 + r, focus))
        for d, r in enumerate(across)
    ]
    total = rows[pl.ds(8 * row, 8)]
    for d, copy in enumerate(second):
        copy.wait_recv()
        total += parts[d]
    sums[...] = total
    third = [send(sums.at[z], ends.at[d], 10 + d, (z * 8 + row, focus)) for d, z in enumerate(along)]
    total = sums[ring]
    for d, copy in enumerate(third):
        copy.wait_recv()
        total += ends[d]
    for i in range(2):
        out[:, R2 * i : R2 * i + R2] = total[i : i + 1] / (total[2 + i : 3 + i] + EPSILON)
    for copy in started + second + third:
        copy.wait_send()


def own_map(terms, blocks):
    vmem = pl.BlockSpec(memory_space=pltpu.VMEM)
    return pl.pallas_call(
        map_kernel,
        out_shape=jax.ShapeDtypeStruct((1, 2 * R2), F32),
        in_specs=[vmem, vmem],
        out_specs=vmem,
        scratch_shapes=[
            pltpu.VMEM((3, LISTED, 512), BF16),
            pltpu.VMEM((64, 4, R2), F32),
            pltpu.VMEM((7, 8, 4, R2), F32),
            pltpu.VMEM((8, 4, R2), F32),
            pltpu.VMEM((7, 4, R2), F32),
            pltpu.SemaphoreType.DMA((34,)),
        ],
        compiler_params=pltpu.CompilerParams(
            has_side_effects=True, vmem_limit_bytes=62 * 2**20, collective_id=1
        ),
        name="phase_rows",
    )(terms, blocks)


def on_device(
    echoes,
    scale_rate,
    migration,
    range_phase,
    azimuth_rate,
    bright_columns,
    line_block,
    line_center,
):
    arrived = corner_turned(echoes, scale_rate, migration, range_phase)
    focused_image, terms = focused(arrived, azimuth_rate, bright_columns, line_center)
    phase_map = own_map(terms, line_block.reshape(1, LISTED))
    return (focused_image, phase_map)


def solution(mesh):
    in_specs = (
        P(None, ("form", "focus"), None),
        P(("form", "focus")),
        P(("form", "focus")),
        P(),
        P(("form", "focus")),
        P("form", None),
        P("form", None, None),
        P("form", None),
    )
    out_specs = (P(None, None, ("form", "focus")), P(("form", "focus"), None))
    return jax.shard_map(
        on_device, mesh=mesh, in_specs=in_specs, out_specs=out_specs, check_vma=False
    )
```

```python
import functools
import math

import jax
import jax.numpy as jnp
import ml_dtypes
import numpy as np
from jax import lax
from jax.experimental import pallas as pl
from jax.experimental.pallas import tpu as pltpu
from jax.sharding import PartitionSpec as P

R1 = 256
R2 = 128
NBLK = 256
AZ = 8192
CHUNKS = 4
LISTED = 32
LINES = 8
MESH = pl.DeviceIdType.MESH
F32 = jnp.float32
BF16 = jnp.bfloat16

TWO_PI = 2.0 * math.pi
EPSILON = 1e-06


def real_blocks(values):
    upper = np.stack([values.real, -values.imag], axis=-2)
    lower = np.stack([values.imag, values.real], axis=-2)
    return np.stack([upper, lower], axis=-4)


def unit(turns):
    return np.exp(2j * np.pi * turns)


def range_tables():
    k = np.arange(R1)
    n = np.arange(R2)
    wide = np.outer(k, k) % R1 / R1
    narrow = np.outer(n, n) % R2 / R2
    first = real_blocks(unit(-wide) / 16).reshape(2 * R1, 2 * R1)
    last = real_blocks(unit(wide) / 16).reshape(2 * R1, 2 * R1)
    inner = real_blocks(unit(-narrow) / math.sqrt(R2)).reshape(2 * R2, 2 * R2).T
    outer = real_blocks(unit(narrow) / math.sqrt(R2)).reshape(2 * R2, 2 * R2).T
    twist = unit(np.outer(k, n) / (R1 * R2))
    length = R1 * R2
    offsets = (k[:, None] * R2 + n[None, :] - length // 2) / length
    bins = k[:, None] + R1 * n[None, :]
    signed = np.where(bins >= length // 2, bins - length, bins) / length
    planes = np.stack([twist.real, twist.imag, offsets * offsets / TWO_PI, signed])
    swap = np.eye(256).reshape(LINES, 2, 16, 256).transpose(2, 1, 0, 3).reshape(256, 256)
    cross = np.eye(256).reshape(16, 16, 256).transpose(1, 0, 2).reshape(256, 256)
    half = [t.astype(ml_dtypes.bfloat16) for t in (first, inner, outer, last, swap, cross)]
    return half + [planes.astype(np.float32)]


def azimuth_tables():
    i = np.arange(16)
    near = np.outer(i, i) / 16
    shift = np.outer(i, i) / 256
    l8, m = np.arange(LINES), np.arange(32)
    eye = np.eye(LINES)

    def widened(turns):
        blocks = real_blocks(np.moveaxis(unit(turns) / 4, -1, 0))
        full = np.einsum("l...atcf,lm->...talfcm", blocks, eye)
        return full.reshape(*full.shape[:-6], 256, 256)

    same = np.zeros(LINES)
    lines = LINES * np.arange(CHUNKS)[:, None] + l8
    first = widened(-(near[None] + shift[:, :, None])[..., None] - same)
    second = widened(-near[None, :, :, None] - (i[:, None] * lines[:, None, :] / 512)[:, :, None, :])
    part = (lines[None] * i[:, None, None] / AZ)[:, None] + (lines * m[:, None, None] / 32)[None]
    wide = real_blocks((unit(-part) / math.sqrt(32)).reshape(16, 32, 32)).reshape(16, 2, 32, 2, CHUNKS, LINES)
    third = np.einsum("kamchl,xy->kxamyhcl", wide, np.eye(4)).reshape(16, 256, 256)
    wide = real_blocks((unit(part) / math.sqrt(32)).transpose(0, 2, 3, 1).reshape(16, 32, 32))
    wide = wide.reshape(16, 2, CHUNKS, LINES, 2, 32)
    fourth = np.einsum("kahlcm,xy->kxhalycm", wide, np.eye(4)).reshape(16, 256, 256)
    fifth = widened(near[None, :, :, None] + (i[:, None] * lines[:, None, :] / 512)[:, None, :, :])
    sixth = widened((near[None] + shift[:, None, :])[..., None] + same)
    return [t.astype(ml_dtypes.bfloat16) for t in (first, second, third, fourth, fifth, sixth)]


def cos_sin(turns):
    rest = turns - jnp.round(turns)
    z = rest * rest
    sine = rest * (6.28316395 + z * (-10.3342826 + z * (5.08377413 - 1.1092177 * z)))
    cosine = 0.99999995 + z * (-4.93479283 + z * (4.05841135 + z * (-1.33187657 + 0.21968961 * z)))
    return 1.0 - 0.5 * (sine * sine), sine * cosine


def dot(a, b):
    return jnp.dot(a, b, preferred_element_type=F32)


def pair(one, other):
    return jnp.concatenate([one.reshape(256, R2), other.reshape(256, R2)], axis=1)


def halves(out):
    out = out.astype(BF16)
    return [out[:, R2 * i : R2 * i + R2].reshape(16, 16, R2) for i in range(2)]


def first_stages(h, r, y, z, first, second):
    def one(s, _):
        out = halves(dot(first[s], pair(r[2 * h, :, s], r[2 * h + 1, :, s])))
        for i in range(2):
            y[2 * h + i, :, s] = out[i]
        return 0

    lax.fori_loop(0, 16, one, 0, unroll=8)
    for c in (2 * h, 2 * h + 1):

        def two(k, _):
            out = halves(dot(second[c], pair(y[c, 2 * k], y[c, 2 * k + 1])))
            for i in range(2):
                z[:, 2 * k + i, c] = out[i]
            return 0

        lax.fori_loop(0, 8, two, 0, unroll=8)


def spectrum(z, third, k, h):
    return dot(third[k], pair(z[pl.ds(8 * h, 4), k], z[pl.ds(8 * h + 4, 4), k]))


def range_kernel(
    x_hbm, rate, shift, phase, *args, talk=True,
):
    sources, out_hbm, tables = args[:9], args[9], args[10:19]
    raw, xbuf, rp, rows, send, got, y, z, in_sem, tab_sem, send_sem, recv_sem, own_sem, out_sem = args[19:]
    first, inner, outer, last, swap, cross, planes, az_first, az_second = tables
    loads = [
        pltpu.make_async_copy(x_hbm.at[:, pl.ds(16 * h, 16)], raw.at[h], in_sem.at[h]) for h in range(2)
    ]
    copies = [pltpu.make_async_copy(a, b, tab_sem.at[i]) for i, (a, b) in enumerate(zip(sources, tables))]
    loads[0].start()
    copies[5].start()
    if talk:
        form = lax.axis_index("form")
        focus = lax.axis_index("focus")
        me = form * 4 + focus
        me_hi, me_lo = lax.div(me, 16), lax.rem(me, 16)
        barrier = pltpu.get_barrier_semaphore()

        others = [focus] + [jnp.where(focus >= 4 - dy, focus + dy - 4, focus + dy) for dy in range(1, 4)]

        def greet(j, _):
            for d in range(8):
                group = form + j + 8 * d
                group = jnp.where(group >= 64, group - 64, group)
                for dy in range(4):

                    def hello():
                        pl.semaphore_signal(
                            barrier, inc=1, device_id=(group, others[dy]), device_id_type=MESH
                        )

                    if d == 0 and dy == 0:
                        pl.when(j > 0)(hello)
                    else:
                        hello()
            return 0

        lax.fori_loop(0, 8, greet, 0)

    for i in (6, 0, 1, 2, 3, 4):
        copies[i].start()
    loads[1].start()
    copies[7].start()
    copies[8].start()
    for i in range(2):
        rp[R2 * i : R2 * i + R2] = phase[pl.ds(i, R2, stride=2), :].T * (1.0 / TWO_PI)
    copies[5].wait()
    def chunk(c, _):
        h = lax.div(c, 2)

        @pl.when(lax.rem(c, 2) == 0)
        def _():
            pltpu.make_async_copy(x_hbm.at[:, pl.ds(16 * h, 16)], raw.at[h], in_sem.at[h]).wait()

            def unfold(t, _):
                cut = [
                    jnp.concatenate(
                        [
                            raw[h, a, :, pl.ds(pl.multiple_of(2048 * t + R2 * i, R2), R2)]
                            for i in range(16)
                        ],
                        axis=0,
                    )
                    for a in range(2)
                ]
                out = dot(cross[...], jnp.concatenate(cut, axis=1)).astype(BF16)
                for a in range(2):
                    xbuf[a, :, pl.ds(pl.multiple_of(16 * t, 16), 16)] = out[
                        :, R2 * a : R2 * a + R2
                    ].reshape(16, 16, R2)
                return 0

            lax.fori_loop(0, 16, unfold, 0, unroll=4)

        @pl.when(c == 0)
        def _():
            for i in (6, 0, 1, 2, 3, 4):
                copies[i].wait()

        half = LINES * lax.rem(c, 2)

        def two_lines(p, _):
            parts = []
            for i in range(2):
                l = 2 * p + i
                cosine, sine = cos_sin(rate[LINES * c + l] * planes[2])
                re = xbuf[0, half + l].astype(F32)
                im = xbuf[1, half + l].astype(F32)
                parts.append(
                    jnp.concatenate(
                        [
                            (re * cosine - im * sine).astype(BF16),
                            (re * sine + im * cosine).astype(BF16),
                        ],
                        axis=0,
                    )
                )
            u = dot(first[...], jnp.concatenate(parts, axis=1))
            parts = []
            for i in range(2):
                lanes = slice(R2 * i, R2 * i + R2)
                re, im = u[:R1, lanes], u[R1:, lanes]
                cosine, sine = planes[0], planes[1]
                twisted = jnp.concatenate(
                    [
                        (re * cosine + im * sine).astype(BF16),
                        (im * cosine - re * sine).astype(BF16),
                    ],
                    axis=1,
                )
                spectrum = dot(twisted, inner[...])
                re, im = spectrum[:, :R2], spectrum[:, R2:]
                cosine, sine = cos_sin(rp[...] + shift[LINES * c + 2 * p + i] * planes[3])
                matched = jnp.concatenate(
                    [
                        (re * cosine + im * sine).astype(BF16),
                        (im * cosine - re * sine).astype(BF16),
                    ],
                    axis=1,
                )
                w = dot(matched, outer[...])
                re, im = w[:, :R2], w[:, R2:]
                cosine, sine = planes[0], planes[1]
                parts.append(
                    jnp.concatenate(
                        [
                            (re * cosine - im * sine).astype(BF16),
                            (re * sine + im * cosine).astype(BF16),
                        ],
                        axis=0,
                    )
                )
            done = dot(last[...], jnp.concatenate(parts, axis=1)).astype(BF16)
            for i in range(2):
                for a in range(2):
                    rows[2 * p + i, a] = done[R1 * a : R1 * a + R1, R2 * i : R2 * i + R2]
            return 0

        lax.fori_loop(0, LINES // 2, two_lines, 0, unroll=4)

        def swapped(t, _):
            cut = [
                rows[:, :, pl.ds(pl.multiple_of(32 * t + 16 * i, 16), 16)].reshape(256, R2)
                for i in range(2)
            ]
            out = dot(swap[...], jnp.concatenate(cut, axis=1)).astype(BF16)
            for i in range(2):
                send[c, pl.ds(32 * t + 16 * i, 16)] = out[:, R2 * i : R2 * i + R2].reshape(16, 16, R2)
            return 0

        lax.fori_loop(0, 8, swapped, 0, unroll=2)
        if not talk:
            return 0

        @pl.when(c == 0)
        def _():
            pl.semaphore_wait(barrier, 255)

        pltpu.make_async_copy(send.at[c, me], got.at[c, me_hi, me_lo], own_sem.at[c]).start()

        def sends(j, _):
            dy = lax.rem(j, 4)
            other = focus + dy
            other = jnp.where(other >= 4, other - 4, other)
            base = form + lax.div(j, 4)
            for dz in (4, 3, 5, 2, 6, 1, 7, 0):
                group = base + 8 * dz
                group = jnp.where(group >= 64, group - 64, group)

                def go():
                    pltpu.make_async_remote_copy(
                        src_ref=send.at[c, group * 4 + other],
                        dst_ref=got.at[c, me_hi, me_lo],
                        send_sem=send_sem,
                        recv_sem=recv_sem.at[c],
                        device_id=(group, other),
                        device_id_type=MESH,
                    ).start()

                if dz == 0:
                    pl.when(j > 0)(go)
                else:
                    go()
            return 0

        lax.fori_loop(0, 32, sends, 0)
        return 0

    lax.fori_loop(0, CHUNKS, chunk, 0)
    for h in range(2):
        if h == 0:
            copies[7].wait()
            copies[8].wait()
        if talk:
            for c in (2 * h, 2 * h + 1):
                pltpu.make_async_copy(send.at[c, 0], got.at[c, 0, 0], own_sem.at[c]).wait()
                pltpu.make_async_copy(
                    send.at[c, pl.ds(0, 255)], send.at[c, pl.ds(0, 255)], recv_sem.at[c]
                ).wait()
        first_stages(h, got, y, z, az_first, az_second)
        pltpu.make_async_copy(
            z.at[:, :, pl.ds(2 * h, 2)], out_hbm.at[:, :, pl.ds(2 * h, 2)], out_sem.at[h]
        ).start()
    if talk:
        pltpu.make_async_copy(send.at[:, pl.ds(0, 255)], send.at[:, pl.ds(0, 255)], send_sem).wait()
    for h in range(2):
        pltpu.make_async_copy(
            z.at[:, :, pl.ds(2 * h, 2)], out_hbm.at[:, :, pl.ds(2 * h, 2)], out_sem.at[h]
        ).wait()


def corner_turned(echoes, rate, shift, range_phase, talk=True):
    phase = range_phase.reshape(R1, R2)
    tables = range_tables() + azimuth_tables()[:2]
    vmem = pl.BlockSpec(memory_space=pltpu.VMEM)
    smem = pl.BlockSpec(memory_space=pltpu.SMEM)
    hbm = pl.BlockSpec(memory_space=pl.ANY)
    return pl.pallas_call(
        functools.partial(range_kernel, talk=talk),
        out_shape=jax.ShapeDtypeStruct((16, 16, CHUNKS, 16, R2), BF16),
        in_specs=[hbm, smem, smem, vmem] + [hbm] * 9,
        out_specs=hbm,
        scratch_shapes=[
            *[pltpu.VMEM(t.shape, t.dtype) for t in tables],
            pltpu.VMEM((2, 2, 16, R1 * R2), BF16),
            pltpu.VMEM((2, 16, R1, R2), BF16),
            pltpu.VMEM((R1, R2), F32),
            pltpu.VMEM((LINES, 2, R1, R2), BF16),
            pltpu.VMEM((CHUNKS, 256, 2 * LINES, R2), BF16),
            pltpu.VMEM((CHUNKS, 16, 16, 16, R2), BF16),
            pltpu.VMEM((CHUNKS, 16, 16, 16, R2), BF16),
            pltpu.VMEM((16, 16, CHUNKS, 16, R2), BF16),
            pltpu.SemaphoreType.DMA((2,)),
            pltpu.SemaphoreType.DMA((9,)),
            pltpu.SemaphoreType.DMA,
            pltpu.SemaphoreType.DMA((CHUNKS,)),
            pltpu.SemaphoreType.DMA((CHUNKS,)),
            pltpu.SemaphoreType.DMA((2,)),
        ],
        compiler_params=pltpu.CompilerParams(
            has_side_effects=True, vmem_limit_bytes=62 * 2**20, **({"collective_id": 0} if talk else {})
        ),
        cost_estimate=pl.CostEstimate(flops=7 * 10**9, bytes_accessed=10**7, transcendentals=0),
        name="range_lines",
    )(echoes, rate, shift, phase, *[jnp.asarray(t) for t in tables])


def azimuth_kernel(
    z_hbm, t3, t4, t5, t6, rate, img_hbm, y, z, back, third, fourth, fifth, sixth, img, sems, tab_sems, out_sem,
):
    def batch(g):
        part = pl.ds(4 * g, 4)
        refs = [(z_hbm.at[:, part], z.at[:, part]), (t3.at[part], third.at[part]), (t4.at[part], fourth.at[part])]
        return [pltpu.make_async_copy(a, b, sems.at[g, i]) for i, (a, b) in enumerate(refs)]

    for g in range(4):
        for copy in batch(g):
            copy.start()
    tables = [
        pltpu.make_async_copy(a, b, tab_sems.at[i])
        for i, (a, b) in enumerate([(t5, fifth), (t6, sixth)])
    ]
    for copy in tables:
        copy.start()
    m = lax.broadcasted_iota(jnp.int32, (32, R2), 0)
    m = jnp.where(m >= 16, m - 32, m).astype(F32) * (1.0 / 32)
    cycles = rate[...] * (1.0 / TWO_PI)

    def filtered(j, _):
        k, h = lax.div(j, 2), lax.rem(j, 2)
        out = spectrum(z, third, k, h)
        columns = []
        for i in range(2):
            rows = []
            for x in range(4):
                re = out[64 * x : 64 * x + 32, R2 * i : R2 * i + R2]
                im = out[64 * x + 32 : 64 * x + 64, R2 * i : R2 * i + R2]
                f = m + (k + 16 * (8 * h + 4 * i + x)).astype(F32) * (1.0 / AZ)
                cosine, sine = cos_sin(f * f * cycles)
                rows.append((re * cosine + im * sine).astype(BF16))
                rows.append((im * cosine - re * sine).astype(BF16))
            columns.append(jnp.concatenate(rows, axis=0))
        out = dot(fourth[k], jnp.concatenate(columns, axis=1)).astype(BF16)
        for i in range(2):
            back[pl.ds(8 * h + 4 * i, 4), k] = out[:, R2 * i : R2 * i + R2].reshape(4, 4, 16, R2)
        return 0

    for g in range(4):
        for copy in batch(g):
            copy.wait()
        lax.fori_loop(8 * g, 8 * g + 8, filtered, 0, unroll=8)
    tables[0].wait()
    tables[1].wait()
    for c in range(CHUNKS):

        def three(k, _):
            out = halves(dot(fifth[c], pair(back[:, 2 * k, c], back[:, 2 * k + 1, c])))
            for i in range(2):
                y[c, :, 2 * k + i] = out[i]
            return 0

        lax.fori_loop(0, 8, three, 0, unroll=8)
    for h in range(2):

        def four(s, _):
            out = dot(sixth[s], pair(y[2 * h, s], y[2 * h + 1, s]))
            out = out.reshape(16, 2, LINES, 2 * R2)
            out = jnp.concatenate([out[..., :R2], out[..., R2:]], axis=2).astype(BF16)
            for a in range(2):
                img[a, :, s, 16 * h : 16 * h + 16] = out[:, a]
            return 0

        if h == 0:
            lax.fori_loop(0, 16, four, 0, unroll=8)
    leaving = []
    for g in range(2):
        lax.fori_loop(8 * g, 8 * g + 8, four, 0, unroll=8)
        part = pl.ds(8 * g, 8)
        leaving.append(pltpu.make_async_copy(img.at[:, :, part], img_hbm.at[:, :, part], out_sem.at[g]))
        leaving[-1].start()
    for copy in leaving:
        copy.wait()


def focused(arrived, rate):
    vmem = pl.BlockSpec(memory_space=pltpu.VMEM)
    hbm = pl.BlockSpec(memory_space=pl.ANY)
    tables = azimuth_tables()[2:]
    return pl.pallas_call(
        azimuth_kernel,
        out_shape=jax.ShapeDtypeStruct((2, 16, 16, 32, R2), BF16),
        in_specs=[hbm] * 5 + [vmem],
        out_specs=hbm,
        scratch_shapes=[
            pltpu.VMEM((4, 16, 16, 16, R2), BF16),
            pltpu.VMEM((16, 16, 4, 16, R2), BF16),
            pltpu.VMEM((16, 16, 4, 16, R2), BF16),
            *[pltpu.VMEM(t.shape, BF16) for t in tables],
            pltpu.VMEM((2, 16, 16, 32, R2), BF16),
            pltpu.SemaphoreType.DMA((4, 3)),
            pltpu.SemaphoreType.DMA((2,)),
            pltpu.SemaphoreType.DMA((2,)),
        ],
        compiler_params=pltpu.CompilerParams(vmem_limit_bytes=62 * 2**20),
        cost_estimate=pl.CostEstimate(flops=15 * 10**9, bytes_accessed=2 * 10**7, transcendentals=0),
        name="azimuth_columns",
    )(arrived, *[jnp.asarray(t) for t in tables], rate[None])


def lines_kernel(
    img_hbm, t1, t2, t3, listed, held, blocks, out, img, r, y, z, v, first, second, third, table, sel, centers, terms,
    got, rows, parts, sums, ends, img_sems, tab_sems, sems,
):
    pieces = [
        pltpu.make_async_copy(img_hbm.at[:, pl.ds(4 * g, 4)], img.at[:, pl.ds(4 * g, 4)], img_sems.at[g])
        for g in range(4)
    ]
    tables = [
        pltpu.make_async_copy(a, b, tab_sems.at[i])
        for i, (a, b) in enumerate([(t1, first), (t2, second), (t3, third)])
    ]
    for copy in pieces + tables:
        copy.start()
    form = lax.axis_index("form")
    focus = lax.axis_index("focus")
    row, ring = lax.rem(form, 8), lax.div(form, 8)

    def wrapped(value, size):
        return jnp.where(value >= size, value - size, value)

    mates = [(form, wrapped(focus + d, 4)) for d in range(1, 4)]
    across = [wrapped(row + d, 8) for d in range(1, 8)]
    along = [wrapped(ring + d, 8) for d in range(1, 8)]
    barrier = pltpu.get_barrier_semaphore()
    for peer in mates + [(ring * 8 + r, focus) for r in across] + [(z * 8 + row, focus) for z in along]:
        pl.semaphore_signal(barrier, inc=1, device_id=peer, device_id_type=MESH)
    place = lax.broadcasted_iota(jnp.int32, (64, LISTED), 0)
    own = (jnp.bitwise_and(place, 7) * 8 + jnp.right_shift(place, 3)) * 4 + focus
    chosen = jnp.where(own == blocks[...], 1.0, 0.0).astype(BF16)
    own = focus * R2
    centers[...] = jnp.zeros((2, R2), jnp.int32) - 1
    centers[0:1, :LISTED] = held[...]
    centers[1:2, :LISTED] = listed[...] - own
    column = lax.broadcasted_iota(jnp.int32, (R2, R2), 0)
    sel[...] = jnp.where(column == centers[1:2], 1.0, 0.0).astype(BF16)

    line = lax.broadcasted_iota(jnp.int32, (256, R2), 0)

    def windowed(t, _):
        hi, lo = lax.div(t, 2), lax.rem(t, 2) * 8
        away = jnp.bitwise_and(line + 256 * t - centers[0:1], AZ - 1)
        away = jnp.minimum(away, AZ - away).astype(F32)
        window = jnp.maximum(1.0 - away * (16.0 / AZ), 0.0)
        parts = [
            (dot(img[a, hi, pl.ds(lo, 8)].reshape(256, R2), sel[...]) * window).reshape(8, 4, 1, LINES, R2)
            for a in range(2)
        ]
        both = jnp.concatenate(parts, axis=2).astype(BF16)
        for c in range(CHUNKS):
            r[c, hi, pl.ds(lo, 8)] = both[:, c].reshape(8, 16, R2)
        return 0

    for g in range(4):
        pieces[g].wait()
        lax.fori_loop(8 * g, 8 * g + 8, windowed, 0, unroll=4)
    for copy in tables:
        copy.wait()
    for h in range(2):
        first_stages(h, r, y, z, first, second)

    def line_spectrum(j, _):
        k, h = lax.div(j, 2), lax.rem(j, 2)
        out = spectrum(z, third, k, h)
        for i in range(2):
            v[pl.ds(8 * h + 4 * i, 4), k] = out[:, R2 * i : R2 * i + R2].reshape(4, 2, 32, R2)
        return 0

    lax.fori_loop(0, 32, line_spectrum, 0, unroll=8)
    end_re, end_im = pltpu.roll(v[0, 0, 0], 31, 0), pltpu.roll(v[0, 0, 1], 31, 0)

    def group(g, _):
        cross = jnp.zeros((32, R2), F32)
        energy = jnp.zeros((32, R2), F32)
        re, im = v[2 * g, 0, 0], v[2 * g, 0, 1]
        for i in range(1, 33):
            k2 = 2 * g + i // 16
            if i == 32:
                k2 = lax.rem(k2, 16)
            next_re, next_im = v[k2, i % 16, 0], v[k2, i % 16, 1]
            if i == 32:
                next_re = jnp.where(g == 7, end_re, next_re)
                next_im = jnp.where(g == 7, end_im, next_im)
            cross += re * next_im - im * next_re
            energy += re * re + im * im
            re, im = next_re, next_im
        table[pl.ds(g, 32, stride=8)] = cross
        table[pl.ds(256 + g, 32, stride=8)] = energy
        return 0

    lax.fori_loop(0, 8, group, 0)
    terms[...] = table[...].T[:LISTED].astype(BF16)
    pl.semaphore_wait(barrier, 17)

    def send(src, dst, i, peer):
        copy = pltpu.make_async_remote_copy(
            src_ref=src,
            dst_ref=dst,
            send_sem=sems.at[2 * i],
            recv_sem=sems.at[2 * i + 1],
            device_id=peer,
            device_id_type=MESH,
        )
        copy.start()
        return copy

    started = [send(terms, got.at[d], d, mates[d]) for d in range(3)]
    for copy in started:
        copy.wait_recv()
    group = terms[...].astype(F32) + got[0].astype(F32) + (got[1].astype(F32) + got[2].astype(F32))
    mine = dot(chosen, group.astype(BF16))
    for i in range(4):
        rows[:, i] = mine[:, R2 * i : R2 * i + R2]
    second = [
        send(rows.at[pl.ds(8 * r, 8)], parts.at[d], 3 + d, (ring * 8 + r, focus))
        for d, r in enumerate(across)
    ]
    total = rows[pl.ds(8 * row, 8)]
    for d, copy in enumerate(second):
        copy.wait_recv()
        total += parts[d]
    sums[...] = total
    third = [send(sums.at[z], ends.at[d], 10 + d, (z * 8 + row, focus)) for d, z in enumerate(along)]
    total = sums[ring]
    for d, copy in enumerate(third):
        copy.wait_recv()
        total += ends[d]
    for i in range(2):
        out[:, R2 * i : R2 * i + R2] = total[i : i + 1] / (total[2 + i : 3 + i] + EPSILON)
    for copy in started + second + third:
        copy.wait_send()


def own_map(image, listed, held, blocks):
    vmem = pl.BlockSpec(memory_space=pltpu.VMEM)
    hbm = pl.BlockSpec(memory_space=pl.ANY)
    tables = azimuth_tables()[:3]
    return pl.pallas_call(
        lines_kernel,
        out_shape=jax.ShapeDtypeStruct((1, 2 * R2), F32),
        in_specs=[hbm] * 4 + [vmem] * 3,
        out_specs=vmem,
        scratch_shapes=[
            pltpu.VMEM((2, 16, 16, 32, R2), BF16),
            pltpu.VMEM((4, 16, 16, 16, R2), BF16),
            pltpu.VMEM((4, 16, 16, 16, R2), BF16),
            pltpu.VMEM((16, 16, 4, 16, R2), BF16),
            pltpu.VMEM((16, 16, 2, 32, R2), F32),
            *[pltpu.VMEM(t.shape, BF16) for t in tables],
            pltpu.VMEM((512, R2), F32),
            pltpu.VMEM((R2, R2), BF16),
            pltpu.VMEM((2, R2), jnp.int32),
            pltpu.VMEM((LISTED, 512), BF16),
            pltpu.VMEM((3, LISTED, 512), BF16),
            pltpu.VMEM((64, 4, R2), F32),
            pltpu.VMEM((7, 8, 4, R2), F32),
            pltpu.VMEM((8, 4, R2), F32),
            pltpu.VMEM((7, 4, R2), F32),
            pltpu.SemaphoreType.DMA((4,)),
            pltpu.SemaphoreType.DMA((3,)),
            pltpu.SemaphoreType.DMA((34,)),
        ],
        compiler_params=pltpu.CompilerParams(
            has_side_effects=True, vmem_limit_bytes=62 * 2**20, collective_id=1
        ),
        name="phase_rows",
    )(image, *[jnp.asarray(t) for t in tables], listed, held, blocks)


def on_device(
    echoes,
    scale_rate,
    migration,
    range_phase,
    azimuth_rate,
    bright_columns,
    line_block,
    line_center,
):
    arrived = corner_turned(echoes, scale_rate, migration, range_phase)
    image = focused(arrived, azimuth_rate)
    phase_map = own_map(image, bright_columns, line_center, line_block.reshape(1, LISTED))
    focused_image = image.reshape(2, AZ, R2)
    return (focused_image, phase_map)


def solution(mesh):
    in_specs = (
        P(None, ("form", "focus"), None),
        P(("form", "focus")),
        P(("form", "focus")),
        P(),
        P(("form", "focus")),
        P("form", None),
        P("form", None, None),
        P("form", None),
    )
    out_specs = (P(None, None, ("form", "focus")), P(("form", "focus"), None))
    return jax.shard_map(
        on_device, mesh=mesh, in_specs=in_specs, out_specs=out_specs, check_vma=False
    )
```
